32 devices in a mesh: expert: 4 (over x, core), tensor: 8 (over z, y).
Axes of the slice: x: 2, y: 2, z: 4, core: 2. Of those that a mesh axis runs over, the one named last changes fastest.
Arguments:
- resid: bfloat16 [2048, 2048], P(('expert', 'tensor')), may hold values from -6 to 6
- contexts: bfloat16 [2048, 4096], P('expert', 'tensor'), may hold values from -6 to 6
- att_routes: int32 [2048, 2], P('expert'), may hold values from 0 to 7, all different within a row
- att_scores: float32 [2048, 2], P('expert'), may hold values from -6 to 6
- att_out_w: bfloat16 [8, 2048, 2048], P(None, 'tensor'), may hold values from -0.125 to 0.125
- norm_gain: bfloat16 [2048], replicated, may hold values from 0.25 to 1.75
- router_w: bfloat16 [2048, 8], replicated, may hold values from -0.125 to 0.125
- mlp_routes: int32 [2048, 2], P(('expert', 'tensor')), may hold values from 0 to 7, all different within a row
- split_rule: int32 [2048, 2], P(('expert', 'tensor')), may hold values from 0 to 2519
- placement: int32 [8], replicated, may hold values from 0 to 7, as said below
- cap_blocks: int32 [8], replicated, may hold values from 1 to 2, as said below
- w_gate_up: bfloat16 [8, 2048, 2, 5632], P('tensor', None, None, 'expert'), as said below
- w_down: bfloat16 [8, 5632, 2048], P('tensor', 'expert'), as said below
- final_gain: bfloat16 [2048], replicated, may hold values from 0.25 to 1.75
Outputs:
- stream_out: bfloat16 [2048, 2048], P(('expert', 'tensor'))
- normalized: bfloat16 [2048, 2048], P(('expert', 'tensor'))
The draws below stay inside these ranges and needn't reach their ends.
Inputs may be any that keep to these rules, and one draw needn't show every extreme that they name: `att_routes`: each row names 2 different experts. `mlp_routes`: each row names 2 different experts. `placement`: every expert is held by at least one slot. `cap_blocks`: some slot accepts 2 blocks. `w_gate_up`: slots that hold the same expert hold equal weights. `w_down`: slots that hold the same expert hold equal weights.
All inputs are finite; a program needn't handle non-finite values.
Results may differ from the reference program's by a relative error of at most 0.023.
Values may be sent and summed in bfloat16 or wider, within the bound.
A program may use at most 64 MiB of HBM per device.

```python
import jax
import jax.numpy as jnp
from jax import lax

D = 2048
CTX = 2048
FF = 5632
E_ATT = 8
E_MLP = 8
TOP = 2
MAXB = 2
ROWS = 64
REPLICAS = 8
SOURCES = 32
TOKENS = 2048
CTXS = 256
BLOCK = 8
CAPM = 16
N_EXPERT = 4
N_TENSOR = 8


def replica_table(key):
    base_key = jax.random.fold_in(key, 101)
    extra = jax.random.randint(jax.random.fold_in(base_key, 1), (REPLICAS - E_MLP,), 0, E_MLP).astype(jnp.int32)
    listed = jnp.concatenate([jnp.arange(E_MLP, dtype=jnp.int32), extra])
    order = jax.random.permutation(jax.random.fold_in(base_key, 2), REPLICAS)
    return listed[order].astype(jnp.int32)


def expert_normal(key, salt, expert_id, shape):
    return jax.random.normal(jax.random.fold_in(jax.random.fold_in(key, salt), expert_id), shape, jnp.float32)


def draw_placement(key, part):
    return replica_table(key)


def draw_w_gate_up(key, part):
    listed = replica_table(key)
    values = jax.vmap(lambda expert_id: expert_normal(key, 202, expert_id, (D, 2, FF)))(listed)
    return (values * D ** (-0.5)).astype(jnp.bfloat16)


def draw_w_down(key, part):
    listed = replica_table(key)
    values = jax.vmap(lambda expert_id: expert_normal(key, 203, expert_id, (FF, D)))(listed)
    return (values * FF ** (-0.5)).astype(jnp.bfloat16)


def draw_cap_blocks(key, part):
    values = jax.random.randint(jax.random.fold_in(key, 303), (REPLICAS,), 1, MAXB + 1)
    chosen_slot = jax.random.randint(jax.random.fold_in(key, 304), (), 0, REPLICAS)
    return jnp.where(jnp.arange(REPLICAS) == chosen_slot, MAXB, values).astype(jnp.int32)


def touch_ends(entries, own_key, low, largest):
    spot = [jax.random.randint(jax.random.fold_in(own_key, axis), (), 0, length) for axis, length in enumerate(entries.shape)]
    main_axis = entries.shape.index(max(entries.shape))
    next_to = spot[:main_axis] + [(spot[main_axis] + 1) % entries.shape[main_axis]] + spot[main_axis + 1:]
    return entries.at[tuple(spot)].set(low).at[tuple(next_to)].set(largest)


def levels(stream_key, dims, pieces, low, largest):
    def one(dim, parts):
        heights = jax.random.uniform(jax.random.fold_in(jax.random.fold_in(stream_key, 6), dim), (parts,), jnp.float32, low / len(pieces), largest / len(pieces))
        return jnp.repeat(jnp.exp(heights), dims[dim] // parts).reshape((-1,) + (1,) * (len(dims) - dim - 1))

    level = one(*pieces[0])
    for cut in pieces[1:]:
        level = level * one(*cut)
    return level


def choose_distinct(stream_key, rows, number_of, top, lift):
    sequence = jax.random.permutation(jax.random.fold_in(stream_key, 1), number_of)
    favour = sequence
    for power in range(3):
        favour = favour * favour // number_of
    favour = favour * lift // number_of
    chance = jax.random.randint(jax.random.fold_in(stream_key, 2), (rows, number_of), 0, 4096) + favour
    sure = jax.random.permutation(jax.random.fold_in(stream_key, 3), rows)[jnp.arange(number_of) % rows]
    chance = jnp.where(jnp.arange(rows)[:, None] == sure[None, :], 1 << 14, chance)
    merit = chance * number_of + jnp.arange(number_of)
    return lax.top_k(merit.astype(jnp.int32), top)[1].astype(jnp.int32)


def gaussian(stream_key, extent, deviation, limit, cuts=(), kind=jnp.bfloat16):
    level = levels(stream_key, extent, cuts, -0.22, 0.18) if cuts else 1.0
    result = jax.random.normal(stream_key, extent, jnp.float32) * deviation * level
    return jnp.minimum(jnp.maximum(result, -limit), limit).astype(kind)


def setup_inputs(seed: int = 0) -> dict:
    key_list = jax.random.split(jax.random.key(seed), 15)
    resid = gaussian(key_list[0], (TOKENS, D), 1.0, 6.0, ((0, 32),))
    contexts = gaussian(key_list[1], (TOKENS, CTX * TOP), 1.0, 6.0, ((0, 4), (1, 8)))
    att_routes = choose_distinct(key_list[2], TOKENS, E_ATT, TOP, 2048)
    att_scores = gaussian(key_list[3], (TOKENS, TOP), 1.5, 6.0, ((0, 4),), jnp.float32)
    att_out_w = gaussian(key_list[4], (E_ATT, CTX, D), CTX ** -0.5, 0.125, ((1, 8),))
    norm_gain = jnp.clip(1.0 + 0.15 * jax.random.normal(key_list[5], (D,), jnp.float32), 0.25, 1.75).astype(jnp.bfloat16)
    router_w = gaussian(key_list[6], (D, E_MLP), D ** -0.5, 0.125)
    mlp_routes = choose_distinct(key_list[7], TOKENS, E_MLP, TOP, 4096)
    split_rule = touch_ends(jax.random.randint(key_list[8], (TOKENS, TOP), 0, 2520), jax.random.fold_in(key_list[8], 1), 0, 2519).astype(jnp.int32)
    placement = draw_placement(jax.random.fold_in(key_list[14], 71), 0)
    cap_blocks = draw_cap_blocks(jax.random.fold_in(key_list[14], 71), 0)
    w_gate_up = draw_w_gate_up(jax.random.fold_in(key_list[14], 71), 0)
    w_down = draw_w_down(jax.random.fold_in(key_list[14], 71), 0)
    final_gain = jnp.clip(1.0 + 0.15 * jax.random.normal(key_list[13], (D,), jnp.float32), 0.25, 1.75).astype(jnp.bfloat16)
    return {"resid": resid, "contexts": contexts, "att_routes": att_routes, "att_scores": att_scores, "att_out_w": att_out_w, "norm_gain": norm_gain, "router_w": router_w, "mlp_routes": mlp_routes, "split_rule": split_rule, "placement": placement, "cap_blocks": cap_blocks, "w_gate_up": w_gate_up, "w_down": w_down, "final_gain": final_gain}


norm_eps = 1e-06

def rms_norm(values, gain):
    scale = lax.rsqrt(lax.optimization_barrier(jnp.mean(values * values, axis=-1, keepdims=True)) + norm_eps)
    return values * scale * gain.astype(values.dtype)

def pair_gates(scores):
    first = jax.nn.sigmoid(scores[:, 0] - scores[:, 1])
    return jnp.stack([first, 1.0 - first], axis=1)

def reference(resid, contexts, att_routes, att_scores, att_out_w, norm_gain, router_w, mlp_routes, split_rule, placement, cap_blocks, w_gate_up, w_down, final_gain):
    token_count = resid.shape[0]
    gate_att = pair_gates(att_scores.astype(jnp.float32))
    chosen = (att_routes[:, :, None] == jnp.arange(E_ATT, dtype=jnp.int32)[None, None, :]).astype(jnp.float32)
    weighted = chosen * gate_att[:, :, None]
    context_slices = contexts.reshape(token_count, N_TENSOR, CTXS, TOP)
    out_slices = att_out_w.reshape(E_ATT, N_TENSOR, CTXS, D)

    def attention_step(running, slice_index):
        context_part = lax.dynamic_index_in_dim(context_slices, slice_index, 1, keepdims=False).astype(jnp.float32)
        mixed = jnp.einsum('tke,tck->tec', weighted, context_part).astype(jnp.bfloat16).reshape(token_count, E_ATT * CTXS)
        weight_part = lax.dynamic_index_in_dim(out_slices, slice_index, 1, keepdims=False).reshape(E_ATT * CTXS, D)
        partial_sum = jnp.dot(mixed, weight_part, preferred_element_type=jnp.float32)
        rounded = lax.optimization_barrier(partial_sum.astype(jnp.bfloat16))
        return (running + rounded.astype(jnp.float32), None)
    attention, _ = lax.scan(attention_step, jnp.zeros((token_count, D), jnp.float32), jnp.arange(N_TENSOR, dtype=jnp.int32))
    stream = (resid.astype(jnp.float32) + attention).astype(jnp.bfloat16)
    normed = rms_norm(stream.astype(jnp.float32), norm_gain).astype(jnp.bfloat16)
    logits = jnp.dot(normed, router_w, preferred_element_type=jnp.float32)
    gate_mlp = pair_gates(jnp.take_along_axis(logits, mlp_routes, axis=1))
    slot_ids = jnp.arange(REPLICAS, dtype=jnp.int32)
    expert_ids = jnp.arange(E_MLP, dtype=jnp.int32)
    copies = lax.optimization_barrier(jnp.sum((placement[None, :] == expert_ids[:, None]).astype(jnp.int32), axis=1)).astype(jnp.int32)
    earlier = lax.optimization_barrier(jnp.sum(((placement[None, :] == placement[:, None]) & (slot_ids[None, :] < slot_ids[:, None])).astype(jnp.int32), axis=1)).astype(jnp.int32)
    route_onehot = (mlp_routes[:, :, None] == expert_ids[None, None, :]).astype(jnp.int32)
    route_copies = lax.optimization_barrier(jnp.sum(route_onehot * copies[None, None, :], axis=2)).astype(jnp.int32)
    replica_rank = jnp.remainder(split_rule, route_copies).astype(jnp.int32)
    match = ((placement[None, None, :] == mlp_routes[:, :, None]) & (earlier[None, None, :] == replica_rank[:, :, None])).astype(jnp.int32)
    replica_slot = lax.optimization_barrier(jnp.sum(match * slot_ids[None, None, :], axis=2)).astype(jnp.int32)
    capacity = (lax.optimization_barrier(jnp.sum(match * cap_blocks[None, None, :], axis=2)) * BLOCK).astype(jnp.int32)
    per_source = match.reshape(SOURCES, ROWS * TOP, REPLICAS)
    before = jnp.cumsum(per_source, axis=1) - per_source
    arrival = lax.optimization_barrier(jnp.sum(before * per_source, axis=2)).astype(jnp.int32).reshape(token_count, TOP)
    is_kept = arrival < capacity
    source_index = (jnp.arange(token_count, dtype=jnp.int32) // ROWS)[:, None]
    position = (replica_slot * (SOURCES * CAPM) + source_index * CAPM + arrival).astype(jnp.int32)
    position = jnp.where(is_kept, position, REPLICAS * SOURCES * CAPM).astype(jnp.int32)
    flat_rows = jnp.broadcast_to(normed[:, None, :], (token_count, TOP, D)).reshape(token_count * TOP, D)
    buffer = jnp.zeros((REPLICAS * SOURCES * CAPM, D), jnp.bfloat16).at[position.reshape(-1)].set(flat_rows, mode='drop')
    stacked = buffer.reshape(REPLICAS, SOURCES * CAPM, D)
    unit_slice = FF // N_EXPERT

    def expert_run(replica):
        rows_in = lax.dynamic_index_in_dim(stacked, replica, 0, keepdims=False)
        gate_up = lax.dynamic_index_in_dim(w_gate_up, replica, 0, keepdims=False).reshape(D, 2 * FF)
        both = jnp.dot(rows_in, gate_up, preferred_element_type=jnp.float32)
        hidden = (jax.nn.silu(both[:, :FF]) * both[:, FF:]).astype(jnp.bfloat16)
        hidden_parts = hidden.reshape(SOURCES * CAPM, N_EXPERT, unit_slice)
        down_parts = lax.dynamic_index_in_dim(w_down, replica, 0, keepdims=False).reshape(N_EXPERT, unit_slice, D)

        def part_step(running, slice_index):
            hidden_part = lax.dynamic_index_in_dim(hidden_parts, slice_index, 1, keepdims=False)
            down_part = lax.dynamic_index_in_dim(down_parts, slice_index, 0, keepdims=False)
            rounded = lax.optimization_barrier(jnp.dot(hidden_part, down_part, preferred_element_type=jnp.float32).astype(jnp.bfloat16))
            return (running + rounded.astype(jnp.float32), None)
        summed, _ = lax.scan(part_step, jnp.zeros((SOURCES * CAPM, D), jnp.float32), jnp.arange(N_EXPERT, dtype=jnp.int32))
        return summed.astype(jnp.bfloat16)
    outputs = lax.map(expert_run, jnp.arange(REPLICAS, dtype=jnp.int32))
    flat_out = outputs.reshape(REPLICAS * SOURCES * CAPM, D)
    safe_index = jnp.where(is_kept, position, 0).astype(jnp.int32)
    fetched = flat_out[safe_index.reshape(-1)].reshape(token_count, TOP, D).astype(jnp.float32)
    factors = gate_mlp * is_kept.astype(jnp.float32)
    expert_mix = fetched[:, 0, :] * factors[:, 0:1] + fetched[:, 1, :] * factors[:, 1:2]
    after = stream.astype(jnp.float32) + expert_mix
    return (after.astype(jnp.bfloat16), rms_norm(after, final_gain).astype(jnp.bfloat16))
```

```python
import jax
import jax.numpy as jnp
from jax import lax
from jax.sharding import PartitionSpec as P

MAXB = 2


norm_eps = 1e-06


def rms_norm(values, gain):
    scale = lax.rsqrt(jnp.mean(values * values, axis=-1, keepdims=True) + norm_eps)
    return values * scale * gain.astype(values.dtype)


def pair_gates(scores):
    first = jax.nn.silu(scores[:, 0:1] * 0.0) * 0.0 + jax.nn.sigmoid(
        scores[:, 0:1] - scores[:, 1:2]
    )
    first = first[:, 0]
    return jnp.stack([first, 1.0 - first], axis=1)


def activate(shard_piece, w_gate_up):
    both = jnp.einsum(
        "tsecd,sdgf->tsecgf", shard_piece, w_gate_up, preferred_element_type=jnp.float32
    )
    hidden = (jax.nn.silu(both[:, :, :, :, 0, :]) * both[:, :, :, :, 1, :]).astype(jnp.bfloat16)
    hidden = jnp.transpose(hidden, (0, 2, 3, 1, 4))
    return hidden.reshape(
        hidden.shape[0] * hidden.shape[1] * hidden.shape[2], hidden.shape[3], hidden.shape[4]
    )


def per_device(
    resid,
    contexts,
    att_routes,
    att_scores,
    att_out_w,
    norm_gain,
    router_w,
    mlp_routes,
    split_rule,
    placement,
    cap_blocks,
    w_gate_up,
    w_down,
    final_gain,
):
    n_tensor = lax.axis_size("tensor")
    row_count = resid.shape[0]
    model_width = resid.shape[1]
    group_rows = contexts.shape[0]
    att_experts = att_out_w.shape[0]
    slice_ctx = att_out_w.shape[1]
    top_count = att_routes.shape[1]
    gate_att = pair_gates(att_scores)
    chosen = (
        att_routes[:, :, None] == jnp.arange(att_experts, dtype=jnp.int32)[None, None, :]
    ).astype(jnp.float32)
    weighted = chosen * gate_att[:, :, None]
    context_part = contexts.reshape(group_rows, slice_ctx, top_count).astype(jnp.float32)
    mixed = (
        jnp.einsum("tke,tck->tec", weighted, context_part)
        .astype(jnp.bfloat16)
        .reshape(group_rows, att_experts * slice_ctx)
    )
    weight_flat = att_out_w.reshape(att_experts * slice_ctx, model_width)
    row_block = mixed
    attention = lax.psum_scatter(
        jnp.dot(row_block, weight_flat, preferred_element_type=jnp.float32).astype(jnp.bfloat16),
        "tensor",
        scatter_dimension=0,
        tiled=True,
    ).astype(jnp.float32)
    stream = (resid.astype(jnp.float32) + attention).astype(jnp.bfloat16)
    normed = rms_norm(stream.astype(jnp.float32), norm_gain).astype(jnp.bfloat16)
    logits = jnp.dot(normed, router_w, preferred_element_type=jnp.float32)
    gate_mlp = pair_gates(jnp.take_along_axis(logits, mlp_routes, axis=1))
    replicas = placement.shape[0]
    slots = w_gate_up.shape[0]
    expert_total = router_w.shape[1]
    block_rows = max(1, row_count * top_count // (2 * replicas))
    capacity_rows = MAXB * block_rows
    slot_ids = jnp.arange(replicas, dtype=jnp.int32)
    expert_ids = jnp.arange(expert_total, dtype=jnp.int32)
    copies = jnp.sum((placement[None, :] == expert_ids[:, None]).astype(jnp.int32), axis=1)
    earlier = jnp.sum(
        (
            (placement[None, :] == placement[:, None]) & (slot_ids[None, :] < slot_ids[:, None])
        ).astype(jnp.int32),
        axis=1,
    )
    route_onehot = (mlp_routes[:, :, None] == expert_ids[None, None, :]).astype(jnp.int32)
    route_copies = jnp.sum(route_onehot * copies[None, None, :], axis=2)
    replica_rank = jnp.remainder(split_rule, route_copies)
    match = (
        (placement[None, None, :] == mlp_routes[:, :, None])
        & (earlier[None, None, :] == replica_rank[:, :, None])
    ).astype(jnp.int32)
    replica_slot = jnp.sum(match * slot_ids[None, None, :], axis=2)
    capacity = jnp.sum(match * cap_blocks[None, None, :], axis=2) * block_rows
    flat_match = match.reshape(row_count * top_count, replicas)
    before = jnp.cumsum(flat_match, axis=0) - flat_match
    arrival = jnp.sum(before * flat_match, axis=1).reshape(row_count, top_count)
    is_kept = arrival < capacity
    holder = replica_slot // slots
    within = replica_slot % slots
    position = within * (n_tensor * capacity_rows) + holder * capacity_rows + arrival
    position = jnp.where(is_kept, position, -1)
    buffer_rows = slots * n_tensor * capacity_rows
    placer = jnp.sum(
        (jnp.arange(buffer_rows, dtype=jnp.int32)[:, None, None] == position[None, :, :]).astype(
            jnp.bfloat16
        ),
        axis=2,
    )
    send_rows = jnp.dot(placer, normed, preferred_element_type=jnp.float32).astype(jnp.bfloat16)
    send_rows = send_rows.reshape(slots, n_tensor, capacity_rows, model_width)
    landed = lax.all_to_all(send_rows, "tensor", split_axis=1, concat_axis=1, tiled=True)
    arrived = lax.all_gather(landed[None], "expert", axis=0, tiled=True)
    hidden = activate(arrived, w_gate_up)
    row_block = hidden
    summed = lax.psum_scatter(
        jnp.einsum("bsf,sfd->bsd", row_block, w_down, preferred_element_type=jnp.float32).astype(
            jnp.bfloat16
        ),
        "expert",
        scatter_dimension=0,
        tiled=True,
    )
    results = summed.reshape(n_tensor, capacity_rows, slots, model_width)
    returned = lax.all_to_all(results, "tensor", split_axis=0, concat_axis=0, tiled=True)
    flat_back = returned.reshape(n_tensor * capacity_rows * slots, model_width)
    back_index = jnp.where(is_kept, holder * (capacity_rows * slots) + arrival * slots + within, 0)
    fetched = (
        jnp.take(flat_back, back_index.reshape(-1), axis=0)
        .reshape(row_count, top_count, model_width)
        .astype(jnp.float32)
    )
    factors = gate_mlp * is_kept.astype(jnp.float32)
    expert_mix = fetched[:, 0, :] * factors[:, 0:1] + fetched[:, 1, :] * factors[:, 1:2]
    after = stream.astype(jnp.float32) + expert_mix
    return (after.astype(jnp.bfloat16), rms_norm(after, final_gain).astype(jnp.bfloat16))


def solution(mesh):
    return jax.shard_map(
        per_device,
        mesh=mesh,
        in_specs=(
            P(("expert", "tensor"), None),
            P("expert", "tensor"),
            P("expert", None),
            P("expert", None),
            P(None, "tensor", None),
            P(),
            P(),
            P(("expert", "tensor"), None),
            P(("expert", "tensor"), None),
            P(),
            P(),
            P("tensor", None, None, "expert"),
            P("tensor", "expert", None),
            P(),
        ),
        out_specs=(P(("expert", "tensor"), None), P(("expert", "tensor"), None)),
        check_vma=False,
    )
```

```python
import functools

import jax
import jax.numpy as jnp
from jax import lax
from jax.experimental import pallas as pl
from jax.experimental.pallas import tpu as pltpu
from jax.sharding import PartitionSpec as P

MESH = pl.DeviceIdType.MESH

MAXB = 2


norm_eps = 1e-06


def rms_norm(values, gain):
    scale = lax.rsqrt(jnp.mean(values * values, axis=-1, keepdims=True) + norm_eps)
    return values * scale * gain.astype(values.dtype)


def pair_gates(scores):
    first = jax.nn.silu(scores[:, 0:1] * 0.0) * 0.0 + jax.nn.sigmoid(
        scores[:, 0:1] - scores[:, 1:2]
    )
    first = first[:, 0]
    return jnp.stack([first, 1.0 - first], axis=1)


def activate(shard_piece, w_gate_up):
    both = jnp.einsum(
        "tsecd,sdgf->tsecgf", shard_piece, w_gate_up, preferred_element_type=jnp.float32
    )
    hidden = (jax.nn.silu(both[:, :, :, :, 0, :]) * both[:, :, :, :, 1, :]).astype(jnp.bfloat16)
    hidden = jnp.transpose(hidden, (0, 2, 3, 1, 4))
    return hidden.reshape(
        hidden.shape[0] * hidden.shape[1] * hidden.shape[2], hidden.shape[3], hidden.shape[4]
    )


def per_device(
    resid,
    contexts,
    att_routes,
    att_scores,
    att_out_w,
    norm_gain,
    router_w,
    mlp_routes,
    split_rule,
    placement,
    cap_blocks,
    w_gate_up,
    w_down,
    final_gain,
):
    n_tensor = lax.axis_size("tensor")
    row_count = resid.shape[0]
    model_width = resid.shape[1]
    group_rows = contexts.shape[0]
    att_experts = att_out_w.shape[0]
    slice_ctx = att_out_w.shape[1]
    top_count = att_routes.shape[1]
    gate_att = pair_gates(att_scores)
    chosen = (
        att_routes[:, :, None] == jnp.arange(att_experts, dtype=jnp.int32)[None, None, :]
    ).astype(jnp.float32)
    weighted = chosen * gate_att[:, :, None]
    context_part = contexts.reshape(group_rows, slice_ctx, top_count).astype(jnp.float32)
    mixed = (
        jnp.einsum("tke,tck->tec", weighted, context_part)
        .astype(jnp.bfloat16)
        .reshape(group_rows, att_experts * slice_ctx)
    )
    weight_flat = att_out_w.reshape(att_experts * slice_ctx, model_width)
    row_block = mixed
    attention = lax.psum_scatter(
        jnp.dot(row_block, weight_flat, preferred_element_type=jnp.float32).astype(jnp.bfloat16),
        "tensor",
        scatter_dimension=0,
        tiled=True,
    ).astype(jnp.float32)
    stream = (resid.astype(jnp.float32) + attention).astype(jnp.bfloat16)
    normed = rms_norm(stream.astype(jnp.float32), norm_gain).astype(jnp.bfloat16)
    logits = jnp.dot(normed, router_w, preferred_element_type=jnp.float32)
    gate_mlp = pair_gates(jnp.take_along_axis(logits, mlp_routes, axis=1))
    replicas = placement.shape[0]
    slots = w_gate_up.shape[0]
    expert_total = router_w.shape[1]
    block_rows = max(1, row_count * top_count // (2 * replicas))
    capacity_rows = MAXB * block_rows
    slot_ids = jnp.arange(replicas, dtype=jnp.int32)
    expert_ids = jnp.arange(expert_total, dtype=jnp.int32)
    copies = jnp.sum((placement[None, :] == expert_ids[:, None]).astype(jnp.int32), axis=1)
    earlier = jnp.sum(
        (
            (placement[None, :] == placement[:, None]) & (slot_ids[None, :] < slot_ids[:, None])
        ).astype(jnp.int32),
        axis=1,
    )
    route_onehot = (mlp_routes[:, :, None] == expert_ids[None, None, :]).astype(jnp.int32)
    route_copies = jnp.sum(route_onehot * copies[None, None, :], axis=2)
    replica_rank = jnp.remainder(split_rule, route_copies)
    match = (
        (placement[None, None, :] == mlp_routes[:, :, None])
        & (earlier[None, None, :] == replica_rank[:, :, None])
    ).astype(jnp.int32)
    replica_slot = jnp.sum(match * slot_ids[None, None, :], axis=2)
    capacity = jnp.sum(match * cap_blocks[None, None, :], axis=2) * block_rows
    flat_match = match.reshape(row_count * top_count, replicas)
    before = jnp.cumsum(flat_match, axis=0) - flat_match
    arrival = jnp.sum(before * flat_match, axis=1).reshape(row_count, top_count)
    is_kept = arrival < capacity
    holder = replica_slot // slots
    within = replica_slot % slots
    position = within * (n_tensor * capacity_rows) + holder * capacity_rows + arrival
    position = jnp.where(is_kept, position, -1)
    buffer_rows = slots * n_tensor * capacity_rows
    placer = jnp.sum(
        (jnp.arange(buffer_rows, dtype=jnp.int32)[:, None, None] == position[None, :, :]).astype(
            jnp.bfloat16
        ),
        axis=2,
    )
    send_rows = jnp.dot(placer, normed, preferred_element_type=jnp.float32).astype(jnp.bfloat16)
    send_rows = send_rows.reshape(slots, n_tensor, capacity_rows, model_width)
    landed = lax.all_to_all(send_rows, "tensor", split_axis=1, concat_axis=1, tiled=True)
    arrived = lax.all_gather(landed[None], "expert", axis=0, tiled=True)
    hidden = activate(arrived, w_gate_up)
    row_block = hidden
    summed = lax.psum_scatter(
        jnp.einsum("bsf,sfd->bsd", row_block, w_down, preferred_element_type=jnp.float32).astype(
            jnp.bfloat16
        ),
        "expert",
        scatter_dimension=0,
        tiled=True,
    )
    results = summed.reshape(n_tensor, capacity_rows, slots, model_width)
    returned = lax.all_to_all(results, "tensor", split_axis=0, concat_axis=0, tiled=True)
    flat_back = returned.reshape(n_tensor * capacity_rows * slots, model_width)
    back_index = jnp.where(is_kept, holder * (capacity_rows * slots) + arrival * slots + within, 0)
    fetched = (
        jnp.take(flat_back, back_index.reshape(-1), axis=0)
        .reshape(row_count, top_count, model_width)
        .astype(jnp.float32)
    )
    factors = gate_mlp * is_kept.astype(jnp.float32)
    expert_mix = fetched[:, 0, :] * factors[:, 0:1] + fetched[:, 1, :] * factors[:, 1:2]
    after = stream.astype(jnp.float32) + expert_mix
    return (after.astype(jnp.bfloat16), rms_norm(after, final_gain).astype(jnp.bfloat16))


def greet(n_e, n_t):
    e, t = lax.axis_index("expert"), lax.axis_index("tensor")
    barrier = pltpu.get_barrier_semaphore()
    for d in range(1, n_t):
        pl.semaphore_signal(
            barrier, inc=1, device_id=(e, lax.rem(t + d, n_t)), device_id_type=MESH
        )
    for d in range(1, n_e):
        pl.semaphore_signal(
            barrier, inc=1, device_id=(lax.rem(e + d, n_e), t), device_id_type=MESH
        )
    pl.semaphore_wait(barrier, n_t + n_e - 2)


def send(src, dst, send_sem, recv_sem, device):
    return pltpu.make_async_remote_copy(
        src_ref=src,
        dst_ref=dst,
        send_sem=send_sem,
        recv_sem=recv_sem,
        device_id=device,
        device_id_type=MESH,
    )


def front_kernel(
    n_e, n_t, n_c, cap,
    ctx_ref, routes_ref, scores_ref, w_hbm, resid_ref, gain_ref, router_ref, pick_ref, placer_ref,
    rows_hbm, stream_ref, gate_ref,
    w, mixed, q_send, q_recv, s_send, s_recv, own, d_send, held,
    w_sem, out_sem, qs, qr, ss, sr, ds, dr, xs, xr, cs, cr, fs, fr,
):
    e, t = lax.axis_index("expert"), lax.axis_index("tensor")
    n_z = n_t // 2
    z, y = t // 2, lax.rem(t, 2)
    other = t + 1 - 2 * y
    cross, sibling = lax.rem(e + 2, 4), e + 1 - 2 * lax.rem(e, 2)
    rows = resid_ref.shape[0]
    cols = w.shape[2]
    slice_ctx = ctx_ref.shape[3] // 2
    experts = w.shape[1] // slice_ctx

    def w_copy(c):
        return pltpu.make_async_copy(
            w_hbm.at[:, pl.ds(c * cols, cols)], w.at[c], w_sem.at[c]
        )

    for c in range(n_c):
        w_copy(c).start()
    greet(n_e, n_t)

    j = lax.broadcasted_iota(jnp.int32, (2 * slice_ctx, slice_ctx), 0)
    f = lax.broadcasted_iota(jnp.int32, (2 * slice_ctx, slice_ctx), 1)
    even = (j == 2 * f).astype(jnp.float32).astype(jnp.bfloat16)
    odd = (j == 2 * f + 1).astype(jnp.float32).astype(jnp.bfloat16)

    def mix_block(b, carry):
        zz, yy = b // 2, lax.rem(b, 2)
        ctx = ctx_ref[zz, yy]
        first = jnp.dot(ctx, even, preferred_element_type=jnp.float32)
        second = jnp.dot(ctx, odd, preferred_element_type=jnp.float32)
        scores = scores_ref[zz, yy]
        routes = routes_ref[zz, yy]
        g0 = jax.nn.sigmoid(scores[:, 0:1] - scores[:, 1:2])
        first = first * g0
        second = second * (1.0 - g0)
        for x in range(experts):
            value = jnp.where(routes[:, 0:1] == x, first, 0.0) + jnp.where(
                routes[:, 1:2] == x, second, 0.0
            )
            mixed[zz, yy, :, x * slice_ctx : (x + 1) * slice_ctx] = value.astype(jnp.bfloat16)
        return carry

    lax.fori_loop(0, n_t, mix_block, 0)

    def q_copy(c):
        return send(q_send.at[c], q_recv.at[c], qs.at[c], qr.at[c], (e, other))

    def s_copy(c, d):
        to = lax.rem(z + d, n_z) * 2 + y
        return send(s_send.at[c, d - 1], s_recv.at[c, d - 1], ss.at[c, d - 1], sr.at[c, d - 1], (e, to))

    def pair_step(c, carry):
        w_copy(c).wait()
        block = mixed[:, 1 - y].reshape(n_z * rows, w.shape[1])
        part = jnp.dot(block, w[c], preferred_element_type=jnp.float32)
        q_send[c] = part.astype(jnp.bfloat16).reshape(n_z, rows, cols)
        q_copy(c).start()
        return carry

    lax.fori_loop(0, n_c, pair_step, 0)

    def own_step(c, carry):
        block = mixed[:, y].reshape(n_z * rows, w.shape[1])
        own[c] = jnp.dot(block, w[c], preferred_element_type=jnp.float32).reshape(n_z, rows, cols)
        q_copy(c).wait_recv()
        for d in range(1, n_z):
            to = lax.rem(z + d, n_z)
            s_send[c, d - 1] = (own[c, to] + q_recv[c, to].astype(jnp.float32)).astype(jnp.bfloat16)
            s_copy(c, d).start()
        return carry

    lax.fori_loop(0, n_c, own_step, 0)

    square = jnp.zeros((rows, 1), jnp.float32)
    for c in range(n_c):
        total = own[c, z] + q_recv[c, z].astype(jnp.float32)
        for d in range(1, n_z):
            s_copy(c, d).wait_recv()
            total += s_recv[c, d - 1].astype(jnp.float32)
        at = slice(c * cols, (c + 1) * cols)
        piece = (resid_ref[:, at].astype(jnp.float32) + total).astype(jnp.bfloat16)
        stream_ref[:, at] = piece
        wide = piece.astype(jnp.float32)
        square += jnp.sum(wide * wide, axis=1, keepdims=True)
    width = resid_ref.shape[1]
    scale = lax.rsqrt(square / width + norm_eps)
    normed = (
        stream_ref[...].astype(jnp.float32) * scale * gain_ref[...].astype(jnp.float32)
    ).astype(jnp.bfloat16)
    picked = jnp.dot(placer_ref[...], normed, preferred_element_type=jnp.float32)
    d_send[...] = picked.astype(jnp.bfloat16).reshape(n_t, cap, width)

    def d_copy(d):
        to = lax.rem(t + d, n_t)
        return send(d_send.at[to], held.at[e, t], ds.at[d], dr.at[d], (e, to))

    for d in range(1, n_t):
        d_copy(d).start()
    held[e, t] = d_send[t]

    def x_copy(d):
        src = held.at[e, lax.rem(t + n_t - d, n_t)]
        return send(src, src, xs.at[d], xr.at[d], (cross, t))

    def c_copy(d):
        src = held.at[e, lax.rem(t + n_t - d, n_t)]
        return send(src, src, cs.at[d], cr.at[d], (sibling, t))

    def f_copy(d):
        src = held.at[cross, lax.rem(t + n_t - d, n_t)]
        return send(src, src, fs.at[d], fr.at[d], (sibling, t))

    for d in range(n_t):
        if d:
            d_copy(d).wait_recv()
        x_copy(d).start()
        c_copy(d).start()

    logits = lax.dot_general(
        normed, router_ref[...], (((1,), (1,)), ((), ())), preferred_element_type=jnp.float32
    )
    gap = jnp.sum(logits * pick_ref[...], axis=1, keepdims=True)
    gate_ref[...] = jnp.broadcast_to(jax.nn.sigmoid(gap), gate_ref.shape)

    for d in range(n_t):
        x_copy(d).wait_recv()
        f_copy(d).start()
    for d in range(n_t):
        c_copy(d).wait_recv()
        f_copy(d).wait_recv()
    out = pltpu.make_async_copy(held, rows_hbm, out_sem)
    out.start()

    def q_end(c, carry):
        q_copy(c).wait_send()
        for d in range(1, n_z):
            s_copy(c, d).wait_send()
        return carry

    lax.fori_loop(0, n_c, q_end, 0)
    for d in range(n_t):
        if d:
            d_copy(d).wait_send()
        x_copy(d).wait_send()
        c_copy(d).wait_send()
        f_copy(d).wait_send()
    out.wait()


def back_kernel(
    n_e, n_t, n_c, cap,
    hidden_ref, w_hbm, stream_ref, gate_ref, take_ref, gain_ref,
    out_ref, normal_ref,
    w, a_send, a_recv, x_send, x_recv, own, r_send, back, after,
    w_sem, as_, ar, xs, xr, rs, rr,
):
    e, t = lax.axis_index("expert"), lax.axis_index("tensor")
    chip, core = e // 2, lax.rem(e, 2)
    cross, sibling = lax.rem(e + 2, 4), e + 1 - 2 * core
    rows = stream_ref.shape[0]
    cols = w.shape[2]
    group = n_t * cap

    def w_copy(c):
        return pltpu.make_async_copy(
            w_hbm.at[:, pl.ds(c * cols, cols)], w.at[c], w_sem.at[c]
        )

    for c in range(n_c):
        w_copy(c).start()
    greet(n_e, n_t)

    def a_copy(c):
        return send(a_send.at[c], a_recv.at[c], as_.at[c], ar.at[c], (sibling, t))

    def x_copy(c):
        return send(x_send.at[c], x_recv.at[c], xs.at[c], xr.at[c], (cross, t))

    def r_copy(c, d):
        to = lax.rem(t + d, n_t)
        return send(r_send.at[c, to], back.at[c, t], rs.at[c, d - 1], rr.at[c, d - 1], (e, to))

    def sibling_step(c, carry):
        w_copy(c).wait()
        block = hidden_ref[:, 1 - core].reshape(2 * group, w.shape[1])
        part = jnp.dot(block, w[c], preferred_element_type=jnp.float32)
        a_send[c] = part.astype(jnp.bfloat16).reshape(2, group, cols)
        a_copy(c).start()
        return carry

    lax.fori_loop(0, n_c, sibling_step, 0)

    def own_step(c, carry):
        block = hidden_ref[:, core].reshape(2 * group, w.shape[1])
        own[c] = jnp.dot(block, w[c], preferred_element_type=jnp.float32).reshape(2, group, cols)
        a_copy(c).wait_recv()
        x_send[c] = (own[c, 1 - chip] + a_recv[c, 1 - chip].astype(jnp.float32)).astype(jnp.bfloat16)
        x_copy(c).start()
        return carry

    lax.fori_loop(0, n_c, own_step, 0)

    def return_step(c, carry):
        x_copy(c).wait_recv()
        total = own[c, chip] + a_recv[c, chip].astype(jnp.float32) + x_recv[c].astype(jnp.float32)
        r_send[c] = total.astype(jnp.bfloat16).reshape(n_t, cap, cols)
        for d in range(1, n_t):
            r_copy(c, d).start()
        back[c, t] = r_send[c, t]
        return carry

    lax.fori_loop(0, n_c, return_step, 0)

    first = gate_ref[:, 0:1]
    square = jnp.zeros((rows, 1), jnp.float32)
    for c in range(n_c):
        for d in range(1, n_t):
            r_copy(c, d).wait_recv()
        came = back[c].reshape(group, cols)
        one = jnp.dot(take_ref[0], came, preferred_element_type=jnp.float32)
        two = jnp.dot(take_ref[1], came, preferred_element_type=jnp.float32)
        at = slice(c * cols, (c + 1) * cols)
        value = stream_ref[:, at].astype(jnp.float32) + (one * first + two * (1.0 - first))
        after[:, at] = value
        out_ref[:, at] = value.astype(jnp.bfloat16)
        square += jnp.sum(value * value, axis=1, keepdims=True)
    scale = lax.rsqrt(square / stream_ref.shape[1] + norm_eps)
    normal_ref[...] = (after[...] * scale * gain_ref[...].astype(jnp.float32)).astype(jnp.bfloat16)

    def end(c, carry):
        a_copy(c).wait_send()
        x_copy(c).wait_send()
        for d in range(1, n_t):
            r_copy(c, d).wait_send()
        return carry

    lax.fori_loop(0, n_c, end, 0)


def assign(mlp_routes, split_rule, placement, cap_blocks, expert_total, block_rows):
    row_count, top_count = mlp_routes.shape
    replicas = placement.shape[0]
    slot_ids = jnp.arange(replicas, dtype=jnp.int32)
    same = placement[None, :] == placement[:, None]
    earlier = jnp.sum((same & (slot_ids[None, :] < slot_ids[:, None])).astype(jnp.int32), axis=1)
    holds = placement[None, None, :] == mlp_routes[:, :, None]
    route_copies = jnp.sum(holds.astype(jnp.int32), axis=2)
    replica_rank = jnp.remainder(split_rule, route_copies)
    match = (holds & (earlier[None, None, :] == replica_rank[:, :, None])).astype(jnp.int32)
    slot = jnp.sum(match * slot_ids[None, None, :], axis=2)
    capacity = jnp.sum(match * cap_blocks[None, None, :], axis=2) * block_rows
    flat_match = match.reshape(row_count * top_count, replicas)
    before = jnp.cumsum(flat_match, axis=0) - flat_match
    arrival = jnp.sum(before * flat_match, axis=1).reshape(row_count, top_count)
    return slot, arrival, arrival < capacity


def fused_device(
    resid, contexts, att_routes, att_scores, att_out_w, norm_gain, router_w, mlp_routes, split_rule,
    placement, cap_blocks, w_gate_up, w_down, final_gain,
):
    n_t, n_e = lax.axis_size("tensor"), lax.axis_size("expert")
    rows, width = resid.shape
    n_z = n_t // 2
    experts, slice_ctx = att_out_w.shape[0], att_out_w.shape[1]
    top = att_routes.shape[1]
    expert_total = router_w.shape[1]
    block_rows = max(1, rows * top // (2 * placement.shape[0]))
    cap = MAXB * block_rows
    unit = w_down.shape[1]
    slot, arrival, is_kept = assign(
        mlp_routes, split_rule, placement, cap_blocks, expert_total, block_rows
    )
    position = jnp.where(is_kept, slot * cap + arrival, -1)
    spots = jnp.arange(n_t * cap, dtype=jnp.int32)
    take = (position.T[:, :, None] == spots[None, None, :]).astype(jnp.bfloat16)
    placer = (
        (spots[:, None] == position[None, :, 0]) | (spots[:, None] == position[None, :, 1])
    ).astype(jnp.bfloat16)
    expert_ids = jnp.arange(expert_total, dtype=jnp.int32)
    pick = (mlp_routes[:, 0:1] == expert_ids[None, :]).astype(jnp.float32) - (
        mlp_routes[:, 1:2] == expert_ids[None, :]
    ).astype(jnp.float32)
    bf16, f32, dma = jnp.bfloat16, jnp.float32, pltpu.SemaphoreType.DMA
    vmem, anywhere = pl.BlockSpec(memory_space=pltpu.VMEM), pl.BlockSpec(memory_space=pl.ANY)

    n_c = 8
    cols = width // n_c
    gathered, stream, gate = pl.pallas_call(
        functools.partial(front_kernel, n_e, n_t, n_c, cap),
        out_shape=(
            jax.ShapeDtypeStruct((n_e, n_t, cap, width), bf16),
            jax.ShapeDtypeStruct((rows, width), bf16),
            jax.ShapeDtypeStruct((rows, 128), f32),
        ),
        in_specs=[vmem, vmem, vmem, anywhere] + [vmem] * 5,
        out_specs=(anywhere, vmem, vmem),
        scratch_shapes=[
            pltpu.VMEM((n_c, experts * slice_ctx, cols), bf16),
            pltpu.VMEM((n_z, 2, rows, experts * slice_ctx), bf16),
            pltpu.VMEM((n_c, n_z, rows, cols), bf16),
            pltpu.VMEM((n_c, n_z, rows, cols), bf16),
            pltpu.VMEM((n_c, n_z - 1, rows, cols), bf16),
            pltpu.VMEM((n_c, n_z - 1, rows, cols), bf16),
            pltpu.VMEM((n_c, n_z, rows, cols), f32),
            pltpu.VMEM((n_t, cap, width), bf16),
            pltpu.VMEM((n_e, n_t, cap, width), bf16),
            dma((n_c,)), dma, dma((n_c,)), dma((n_c,)),
            dma((n_c, n_z - 1)), dma((n_c, n_z - 1)),
        ] + [dma((n_t,))] * 8,
        compiler_params=pltpu.CompilerParams(
            collective_id=1, has_side_effects=True, vmem_limit_bytes=44 * 2**20
        ),
    )(
        contexts.reshape(n_z, 2, rows, top * slice_ctx),
        att_routes.reshape(n_z, 2, rows, top),
        att_scores.reshape(n_z, 2, rows, top),
        att_out_w.reshape(experts * slice_ctx, width),
        resid,
        norm_gain.reshape(1, width),
        router_w.T,
        pick,
        placer,
    )
    hidden = activate(gathered[:, None], w_gate_up)
    n_d = 4
    wide = width // n_d
    group = n_t * cap
    return pl.pallas_call(
        functools.partial(back_kernel, n_e, n_t, n_d, cap),
        out_shape=(jax.ShapeDtypeStruct((rows, width), bf16),) * 2,
        in_specs=[vmem, anywhere] + [vmem] * 4,
        out_specs=(vmem, vmem),
        scratch_shapes=[
            pltpu.VMEM((n_d, unit, wide), bf16),
            pltpu.VMEM((n_d, 2, group, wide), bf16),
            pltpu.VMEM((n_d, 2, group, wide), bf16),
            pltpu.VMEM((n_d, group, wide), bf16),
            pltpu.VMEM((n_d, group, wide), bf16),
            pltpu.VMEM((n_d, 2, group, wide), f32),
            pltpu.VMEM((n_d, n_t, cap, wide), bf16),
            pltpu.VMEM((n_d, n_t, cap, wide), bf16),
            pltpu.VMEM((rows, width), f32),
            dma((n_d,)), dma((n_d,)), dma((n_d,)), dma((n_d,)), dma((n_d,)),
            dma((n_d, n_t - 1)), dma((n_d, n_t - 1)),
        ],
        compiler_params=pltpu.CompilerParams(
            collective_id=2, has_side_effects=True, vmem_limit_bytes=44 * 2**20
        ),
    )(
        hidden.reshape(n_e // 2, 2, group, unit),
        w_down.reshape(unit, width),
        stream,
        gate,
        take,
        final_gain.reshape(1, width),
    )


def choose(*args):
    n_t, n_e = lax.axis_size("tensor"), lax.axis_size("expert")
    resid, placement = args[0], args[9]
    replicas = placement.shape[0]
    cap = MAXB * max(1, resid.shape[0] * args[2].shape[1] // (2 * replicas))
    if n_e == 4 and n_t % 2 == 0 and n_t <= 8 and replicas == n_t and cap % 16 == 0:
        return fused_device(*args)
    return per_device(*args)


def solution(mesh):
    return jax.shard_map(
        choose,
        mesh=mesh,
        in_specs=(
            P(("expert", "tensor"), None),
            P("expert", "tensor"),
            P("expert", None),
            P("expert", None),
            P(None, "tensor", None),
            P(),
            P(),
            P(("expert", "tensor"), None),
            P(("expert", "tensor"), None),
            P(),
            P(),
            P("tensor", None, None, "expert"),
            P("tensor", "expert", None),
            P(),
        ),
        out_specs=(P(("expert", "tensor"), None), P(("expert", "tensor"), None)),
        check_vma=False,
    )
```

```python
import functools

import jax
import jax.numpy as jnp
from jax import lax
from jax.experimental import pallas as pl
from jax.experimental.pallas import tpu as pltpu
from jax.sharding import PartitionSpec as P

MESH = pl.DeviceIdType.MESH

MAXB = 2


norm_eps = 1e-06


def rms_norm(values, gain):
    scale = lax.rsqrt(jnp.mean(values * values, axis=-1, keepdims=True) + norm_eps)
    return values * scale * gain.astype(values.dtype)


def pair_gates(scores):
    first = jax.nn.silu(scores[:, 0:1] * 0.0) * 0.0 + jax.nn.sigmoid(
        scores[:, 0:1] - scores[:, 1:2]
    )
    first = first[:, 0]
    return jnp.stack([first, 1.0 - first], axis=1)


def activate(shard_piece, w_gate_up):
    both = jnp.einsum(
        "tsecd,sdgf->tsecgf", shard_piece, w_gate_up, preferred_element_type=jnp.float32
    )
    hidden = (jax.nn.silu(both[:, :, :, :, 0, :]) * both[:, :, :, :, 1, :]).astype(jnp.bfloat16)
    hidden = jnp.transpose(hidden, (0, 2, 3, 1, 4))
    return hidden.reshape(
        hidden.shape[0] * hidden.shape[1] * hidden.shape[2], hidden.shape[3], hidden.shape[4]
    )


def per_device(
    resid,
    contexts,
    att_routes,
    att_scores,
    att_out_w,
    norm_gain,
    router_w,
    mlp_routes,
    split_rule,
    placement,
    cap_blocks,
    w_gate_up,
    w_down,
    final_gain,
):
    n_tensor = lax.axis_size("tensor")
    row_count = resid.shape[0]
    model_width = resid.shape[1]
    group_rows = contexts.shape[0]
    att_experts = att_out_w.shape[0]
    slice_ctx = att_out_w.shape[1]
    top_count = att_routes.shape[1]
    gate_att = pair_gates(att_scores)
    chosen = (
        att_routes[:, :, None] == jnp.arange(att_experts, dtype=jnp.int32)[None, None, :]
    ).astype(jnp.float32)
    weighted = chosen * gate_att[:, :, None]
    context_part = contexts.reshape(group_rows, slice_ctx, top_count).astype(jnp.float32)
    mixed = (
        jnp.einsum("tke,tck->tec", weighted, context_part)
        .astype(jnp.bfloat16)
        .reshape(group_rows, att_experts * slice_ctx)
    )
    weight_flat = att_out_w.reshape(att_experts * slice_ctx, model_width)
    row_block = mixed
    attention = lax.psum_scatter(
        jnp.dot(row_block, weight_flat, preferred_element_type=jnp.float32).astype(jnp.bfloat16),
        "tensor",
        scatter_dimension=0,
        tiled=True,
    ).astype(jnp.float32)
    stream = (resid.astype(jnp.float32) + attention).astype(jnp.bfloat16)
    normed = rms_norm(stream.astype(jnp.float32), norm_gain).astype(jnp.bfloat16)
    logits = jnp.dot(normed, router_w, preferred_element_type=jnp.float32)
    gate_mlp = pair_gates(jnp.take_along_axis(logits, mlp_routes, axis=1))
    replicas = placement.shape[0]
    slots = w_gate_up.shape[0]
    expert_total = router_w.shape[1]
    block_rows = max(1, row_count * top_count // (2 * replicas))
    capacity_rows = MAXB * block_rows
    slot_ids = jnp.arange(replicas, dtype=jnp.int32)
    expert_ids = jnp.arange(expert_total, dtype=jnp.int32)
    copies = jnp.sum((placement[None, :] == expert_ids[:, None]).astype(jnp.int32), axis=1)
    earlier = jnp.sum(
        (
            (placement[None, :] == placement[:, None]) & (slot_ids[None, :] < slot_ids[:, None])
        ).astype(jnp.int32),
        axis=1,
    )
    route_onehot = (mlp_routes[:, :, None] == expert_ids[None, None, :]).astype(jnp.int32)
    route_copies = jnp.sum(route_onehot * copies[None, None, :], axis=2)
    replica_rank = jnp.remainder(split_rule, route_copies)
    match = (
        (placement[None, None, :] == mlp_routes[:, :, None])
        & (earlier[None, None, :] == replica_rank[:, :, None])
    ).astype(jnp.int32)
    replica_slot = jnp.sum(match * slot_ids[None, None, :], axis=2)
    capacity = jnp.sum(match * cap_blocks[None, None, :], axis=2) * block_rows
    flat_match = match.reshape(row_count * top_count, replicas)
    before = jnp.cumsum(flat_match, axis=0) - flat_match
    arrival = jnp.sum(before * flat_match, axis=1).reshape(row_count, top_count)
    is_kept = arrival < capacity
    holder = replica_slot // slots
    within = replica_slot % slots
    position = within * (n_tensor * capacity_rows) + holder * capacity_rows + arrival
    position = jnp.where(is_kept, position, -1)
    buffer_rows = slots * n_tensor * capacity_rows
    placer = jnp.sum(
        (jnp.arange(buffer_rows, dtype=jnp.int32)[:, None, None] == position[None, :, :]).astype(
            jnp.bfloat16
        ),
        axis=2,
    )
    send_rows = jnp.dot(placer, normed, preferred_element_type=jnp.float32).astype(jnp.bfloat16)
    send_rows = send_rows.reshape(slots, n_tensor, capacity_rows, model_width)
    landed = lax.all_to_all(send_rows, "tensor", split_axis=1, concat_axis=1, tiled=True)
    arrived = lax.all_gather(landed[None], "expert", axis=0, tiled=True)
    hidden = activate(arrived, w_gate_up)
    row_block = hidden
    summed = lax.psum_scatter(
        jnp.einsum("bsf,sfd->bsd", row_block, w_down, preferred_element_type=jnp.float32).astype(
            jnp.bfloat16
        ),
        "expert",
        scatter_dimension=0,
        tiled=True,
    )
    results = summed.reshape(n_tensor, capacity_rows, slots, model_width)
    returned = lax.all_to_all(results, "tensor", split_axis=0, concat_axis=0, tiled=True)
    flat_back = returned.reshape(n_tensor * capacity_rows * slots, model_width)
    back_index = jnp.where(is_kept, holder * (capacity_rows * slots) + arrival * slots + within, 0)
    fetched = (
        jnp.take(flat_back, back_index.reshape(-1), axis=0)
        .reshape(row_count, top_count, model_width)
        .astype(jnp.float32)
    )
    factors = gate_mlp * is_kept.astype(jnp.float32)
    expert_mix = fetched[:, 0, :] * factors[:, 0:1] + fetched[:, 1, :] * factors[:, 1:2]
    after = stream.astype(jnp.float32) + expert_mix
    return (after.astype(jnp.bfloat16), rms_norm(after, final_gain).astype(jnp.bfloat16))


def greet(n_e, n_t):
    e, t = lax.axis_index("expert"), lax.axis_index("tensor")
    barrier = pltpu.get_barrier_semaphore()
    for d in range(1, n_t):
        pl.semaphore_signal(
            barrier, inc=1, device_id=(e, lax.rem(t + d, n_t)), device_id_type=MESH
        )
    for d in range(1, n_e):
        pl.semaphore_signal(
            barrier, inc=1, device_id=(lax.rem(e + d, n_e), t), device_id_type=MESH
        )
    pl.semaphore_wait(barrier, n_t + n_e - 2)


def send(src, dst, send_sem, recv_sem, device):
    return pltpu.make_async_remote_copy(
        src_ref=src,
        dst_ref=dst,
        send_sem=send_sem,
        recv_sem=recv_sem,
        device_id=device,
        device_id_type=MESH,
    )


def column(row):
    n = row.shape[1]
    i = lax.broadcasted_iota(jnp.int32, (n, n), 0)
    j = lax.broadcasted_iota(jnp.int32, (n, n), 1)
    return jnp.sum(jnp.where(i == j, row, 0.0), axis=1, keepdims=True)


def assign(routes, splits, place_ref, blocks_ref, block_rows, cap):
    replicas = place_ref.shape[0]
    place = [place_ref[r] for r in range(replicas)]
    limit = [(blocks_ref[r] * block_rows).astype(jnp.float32) for r in range(replicas)]
    earlier = [
        sum(((place[q] == place[r]).astype(jnp.int32) for q in range(r)), jnp.int32(0)).astype(
            jnp.float32
        )
        for r in range(replicas)
    ]
    place = [p.astype(jnp.float32) for p in place]
    rows = routes[0].shape[0]
    lane = lax.broadcasted_iota(jnp.int32, (rows, replicas), 1)
    matches, slots, limits = [], [], []
    for route, split in zip(routes, splits):
        held_by = [(route == p).astype(jnp.float32) for p in place]
        copies = sum(held_by)
        rank = split - copies * jnp.floor((split + 0.5) / copies)
        hits = [h * (rank == q).astype(jnp.float32) for h, q in zip(held_by, earlier)]
        match = jnp.zeros((rows, replicas), jnp.float32)
        for r, hit in enumerate(hits):
            match += jnp.where(lane == r, hit, 0.0)
        matches.append(match)
        slots.append(sum(hit * float(r) for r, hit in enumerate(hits)))
        limits.append(sum(hit * m for hit, m in zip(hits, limit)))
    i = lax.broadcasted_iota(jnp.int32, (rows, rows), 0)
    j = lax.broadcasted_iota(jnp.int32, (rows, rows), 1)
    lower = (j < i).astype(jnp.float32)
    before = jnp.dot(lower, matches[0] + matches[1], preferred_element_type=jnp.float32)
    befores = (before, before + matches[0])
    spot = lax.broadcasted_iota(jnp.int32, (rows, replicas * cap), 1).astype(jnp.float32)
    taken = []
    for k in range(2):
        arrival = jnp.sum(befores[k] * matches[k], axis=1, keepdims=True)
        position = jnp.where(arrival < limits[k], slots[k] * cap + arrival, -1.0)
        taken.append((spot == position).astype(jnp.float32))
    return taken


def front_kernel(
    n_e, n_t, n_c, cap,
    ctx_ref, routes_ref, scores_ref, w_hbm, resid_ref, gain_ref, router_ref,
    chosen_ref, split_ref, place_ref, blocks_ref,
    rows_hbm, stream_ref, gate_ref, take_ref,
    w, mixed, q_send, q_recv, s_send, s_recv, own, d_send, held,
    w_sem, out_sem, qs, qr, ss, sr, ds, dr, xs, xr, cs, cr, fs, fr,
):
    e, t = lax.axis_index("expert"), lax.axis_index("tensor")
    n_z = n_t // 2
    z, y = t // 2, lax.rem(t, 2)
    other = t + 1 - 2 * y
    cross, sibling = lax.rem(e + 2, 4), e + 1 - 2 * lax.rem(e, 2)
    rows = resid_ref.shape[0]
    cols = w.shape[2]
    slice_ctx = ctx_ref.shape[3] // 2
    experts = w.shape[1] // slice_ctx

    def w_copy(c):
        return pltpu.make_async_copy(
            w_hbm.at[:, pl.ds(c * cols, cols)], w.at[c], w_sem.at[c]
        )

    for c in range(n_c):
        w_copy(c).start()
    greet(n_e, n_t)

    j = lax.broadcasted_iota(jnp.int32, (2 * slice_ctx, slice_ctx), 0)
    f = lax.broadcasted_iota(jnp.int32, (2 * slice_ctx, slice_ctx), 1)
    even = (j == 2 * f).astype(jnp.float32).astype(jnp.bfloat16)
    odd = (j == 2 * f + 1).astype(jnp.float32).astype(jnp.bfloat16)

    def mix_block(zz, carry):
        ctx = ctx_ref[zz].reshape(2 * rows, 2 * slice_ctx)
        first = jnp.dot(ctx, even, preferred_element_type=jnp.float32)
        second = jnp.dot(ctx, odd, preferred_element_type=jnp.float32)
        at = pl.ds(pl.multiple_of(zz * 2 * rows, 2 * rows), 2 * rows)
        scores = scores_ref[:, at]
        routes = routes_ref[:, at].astype(jnp.float32)
        g0 = column(jax.nn.sigmoid(scores[0:1] - scores[1:2]))
        r0, r1 = column(routes[0:1]), column(routes[1:2])
        first = first * g0
        second = second * (1.0 - g0)
        for x in range(experts):
            value = jnp.where(r0 == x, first, 0.0) + jnp.where(r1 == x, second, 0.0)
            mixed[zz, :, :, x * slice_ctx : (x + 1) * slice_ctx] = value.astype(
                jnp.bfloat16
            ).reshape(2, rows, slice_ctx)
        return carry

    lax.fori_loop(0, n_z, mix_block, 0)

    def q_copy(c):
        return send(q_send.at[c], q_recv.at[c], qs.at[c], qr.at[c], (e, other))

    def s_copy(c, d):
        to = lax.rem(z + d, n_z) * 2 + y
        return send(s_send.at[c, d - 1], s_recv.at[c, d - 1], ss.at[c, d - 1], sr.at[c, d - 1], (e, to))

    def pair_step(c, carry):
        w_copy(c).wait()
        block = mixed[:, 1 - y].reshape(n_z * rows, w.shape[1])
        part = jnp.dot(block, w[c], preferred_element_type=jnp.float32)
        q_send[c] = part.astype(jnp.bfloat16).reshape(n_z, rows, cols)
        q_copy(c).start()
        return carry

    lax.fori_loop(0, n_c, pair_step, 0)

    routes = [column(chosen_ref[k : k + 1].astype(jnp.float32)) for k in range(2)]
    splits = [column(split_ref[k : k + 1].astype(jnp.float32)) for k in range(2)]
    taken = assign(routes, splits, place_ref, blocks_ref, cap // MAXB, cap)
    for k in range(2):
        take_ref[k] = taken[k].astype(jnp.bfloat16)

    def own_step(c, carry):
        block = mixed[:, y].reshape(n_z * rows, w.shape[1])
        own[c] = jnp.dot(block, w[c], preferred_element_type=jnp.float32).reshape(n_z, rows, cols)
        q_copy(c).wait_recv()
        for d in range(1, n_z):
            to = lax.rem(z + d, n_z)
            s_send[c, d - 1] = (own[c, to] + q_recv[c, to].astype(jnp.float32)).astype(jnp.bfloat16)
            s_copy(c, d).start()
        return carry

    lax.fori_loop(0, n_c, own_step, 0)

    square = jnp.zeros((rows, 1), jnp.float32)
    for c in range(n_c):
        total = own[c, z] + q_recv[c, z].astype(jnp.float32)
        for d in range(1, n_z):
            s_copy(c, d).wait_recv()
            total += s_recv[c, d - 1].astype(jnp.float32)
        at = slice(c * cols, (c + 1) * cols)
        piece = (resid_ref[:, at].astype(jnp.float32) + total).astype(jnp.bfloat16)
        stream_ref[:, at] = piece
        wide = piece.astype(jnp.float32)
        square += jnp.sum(wide * wide, axis=1, keepdims=True)
    width = resid_ref.shape[1]
    scale = lax.rsqrt(square / width + norm_eps)
    normed = (
        stream_ref[...].astype(jnp.float32) * scale * gain_ref[...].astype(jnp.float32)
    ).astype(jnp.bfloat16)
    picked = lax.dot_general(
        (taken[0] + taken[1]).astype(jnp.bfloat16),
        normed,
        (((0,), (0,)), ((), ())),
        preferred_element_type=jnp.float32,
    )
    d_send[...] = picked.astype(jnp.bfloat16).reshape(n_t, cap, width)

    def d_copy(d):
        to = lax.rem(t + d, n_t)
        return send(d_send.at[to], held.at[e, t], ds.at[d], dr.at[d], (e, to))

    for d in range(1, n_t):
        d_copy(d).start()
    held[e, t] = d_send[t]

    def x_copy(d):
        src = held.at[e, lax.rem(t + n_t - d, n_t)]
        return send(src, src, xs.at[d], xr.at[d], (cross, t))

    def c_copy(d):
        src = held.at[e, lax.rem(t + n_t - d, n_t)]
        return send(src, src, cs.at[d], cr.at[d], (sibling, t))

    def f_copy(d):
        src = held.at[cross, lax.rem(t + n_t - d, n_t)]
        return send(src, src, fs.at[d], fr.at[d], (sibling, t))

    for d in range(n_t):
        if d:
            d_copy(d).wait_recv()
        x_copy(d).start()
        c_copy(d).start()

    logits = lax.dot_general(
        normed, router_ref[...], (((1,), (1,)), ((), ())), preferred_element_type=jnp.float32
    )
    expert = lax.broadcasted_iota(jnp.int32, logits.shape, 1).astype(jnp.float32)
    pick = (expert == routes[0]).astype(jnp.float32) - (expert == routes[1]).astype(jnp.float32)
    gap = jnp.sum(logits * pick, axis=1, keepdims=True)
    gate_ref[...] = jnp.broadcast_to(jax.nn.sigmoid(gap), gate_ref.shape)

    for d in range(n_t):
        x_copy(d).wait_recv()
        f_copy(d).start()
    for d in range(n_t):
        c_copy(d).wait_recv()
        f_copy(d).wait_recv()
    out = pltpu.make_async_copy(held, rows_hbm, out_sem)
    out.start()

    def q_end(c, carry):
        q_copy(c).wait_send()
        for d in range(1, n_z):
            s_copy(c, d).wait_send()
        return carry

    lax.fori_loop(0, n_c, q_end, 0)
    for d in range(n_t):
        if d:
            d_copy(d).wait_send()
        x_copy(d).wait_send()
        c_copy(d).wait_send()
        f_copy(d).wait_send()
    out.wait()


def back_kernel(
    n_e, n_t, n_c, cap,
    hidden_ref, w_hbm, stream_ref, gate_ref, take_ref, gain_ref,
    out_ref, normal_ref,
    w, a_send, a_recv, x_send, x_recv, own, r_send, back, after,
    w_sem, as_, ar, xs, xr, rs, rr,
):
    e, t = lax.axis_index("expert"), lax.axis_index("tensor")
    chip, core = e // 2, lax.rem(e, 2)
    cross, sibling = lax.rem(e + 2, 4), e + 1 - 2 * core
    rows = stream_ref.shape[0]
    cols = w.shape[2]
    group = n_t * cap

    def w_copy(c):
        return pltpu.make_async_copy(
            w_hbm.at[:, pl.ds(c * cols, cols)], w.at[c], w_sem.at[c]
        )

    for c in range(n_c):
        w_copy(c).start()
    greet(n_e, n_t)

    def a_copy(c):
        return send(a_send.at[c], a_recv.at[c], as_.at[c], ar.at[c], (sibling, t))

    def x_copy(c):
        return send(x_send.at[c], x_recv.at[c], xs.at[c], xr.at[c], (cross, t))

    def r_copy(c, d):
        to = lax.rem(t + d, n_t)
        return send(r_send.at[c, to], back.at[c, t], rs.at[c, d - 1], rr.at[c, d - 1], (e, to))

    def sibling_step(c, carry):
        w_copy(c).wait()
        block = hidden_ref[:, 1 - core].reshape(2 * group, w.shape[1])
        part = jnp.dot(block, w[c], preferred_element_type=jnp.float32)
        a_send[c] = part.astype(jnp.bfloat16).reshape(2, group, cols)
        a_copy(c).start()
        return carry

    lax.fori_loop(0, n_c, sibling_step, 0)

    def own_step(c, carry):
        block = hidden_ref[:, core].reshape(2 * group, w.shape[1])
        own[c] = jnp.dot(block, w[c], preferred_element_type=jnp.float32).reshape(2, group, cols)
        a_copy(c).wait_recv()
        x_send[c] = (own[c, 1 - chip] + a_recv[c, 1 - chip].astype(jnp.float32)).astype(jnp.bfloat16)
        x_copy(c).start()
        return carry

    lax.fori_loop(0, n_c, own_step, 0)

    def return_step(c, carry):
        x_copy(c).wait_recv()
        total = own[c, chip] + a_recv[c, chip].astype(jnp.float32) + x_recv[c].astype(jnp.float32)
        r_send[c] = total.astype(jnp.bfloat16).reshape(n_t, cap, cols)
        for d in range(1, n_t):
            r_copy(c, d).start()
        back[c, t] = r_send[c, t]
        return carry

    lax.fori_loop(0, n_c, return_step, 0)

    first = gate_ref[:, 0:1]
    square = jnp.zeros((rows, 1), jnp.float32)
    for c in range(n_c):
        for d in range(1, n_t):
            r_copy(c, d).wait_recv()
        came = back[c].reshape(group, cols)
        one = jnp.dot(take_ref[0], came, preferred_element_type=jnp.float32)
        two = jnp.dot(take_ref[1], came, preferred_element_type=jnp.float32)
        at = slice(c * cols, (c + 1) * cols)
        value = stream_ref[:, at].astype(jnp.float32) + (one * first + two * (1.0 - first))
        after[:, at] = value
        out_ref[:, at] = value.astype(jnp.bfloat16)
        square += jnp.sum(value * value, axis=1, keepdims=True)
    scale = lax.rsqrt(square / stream_ref.shape[1] + norm_eps)
    normal_ref[...] = (after[...] * scale * gain_ref[...].astype(jnp.float32)).astype(jnp.bfloat16)

    def end(c, carry):
        a_copy(c).wait_send()
        x_copy(c).wait_send()
        for d in range(1, n_t):
            r_copy(c, d).wait_send()
        return carry

    lax.fori_loop(0, n_c, end, 0)


def fused_device(
    resid, contexts, att_routes, att_scores, att_out_w, norm_gain, router_w, mlp_routes, split_rule,
    placement, cap_blocks, w_gate_up, w_down, final_gain,
):
    n_t, n_e = lax.axis_size("tensor"), lax.axis_size("expert")
    rows, width = resid.shape
    n_z = n_t // 2
    experts, slice_ctx = att_out_w.shape[0], att_out_w.shape[1]
    top = att_routes.shape[1]
    cap = MAXB * max(1, rows * top // (2 * placement.shape[0]))
    unit = w_down.shape[1]
    bf16, f32, dma = jnp.bfloat16, jnp.float32, pltpu.SemaphoreType.DMA
    smem = pl.BlockSpec(memory_space=pltpu.SMEM)
    vmem, anywhere = pl.BlockSpec(memory_space=pltpu.VMEM), pl.BlockSpec(memory_space=pl.ANY)

    n_c = 8
    cols = width // n_c
    gathered, stream, gate, take = pl.pallas_call(
        functools.partial(front_kernel, n_e, n_t, n_c, cap),
        out_shape=(
            jax.ShapeDtypeStruct((n_e, n_t, cap, width), bf16),
            jax.ShapeDtypeStruct((rows, width), bf16),
            jax.ShapeDtypeStruct((rows, 128), f32),
            jax.ShapeDtypeStruct((top, rows, n_t * cap), bf16),
        ),
        in_specs=[vmem, vmem, vmem, anywhere] + [vmem] * 5 + [smem] * 2,
        out_specs=(anywhere, vmem, vmem, vmem),
        scratch_shapes=[
            pltpu.VMEM((n_c, experts * slice_ctx, cols), bf16),
            pltpu.VMEM((n_z, 2, rows, experts * slice_ctx), bf16),
            pltpu.VMEM((n_c, n_z, rows, cols), bf16),
            pltpu.VMEM((n_c, n_z, rows, cols), bf16),
            pltpu.VMEM((n_c, n_z - 1, rows, cols), bf16),
            pltpu.VMEM((n_c, n_z - 1, rows, cols), bf16),
            pltpu.VMEM((n_c, n_z, rows, cols), f32),
            pltpu.VMEM((n_t, cap, width), bf16),
            pltpu.VMEM((n_e, n_t, cap, width), bf16),
            dma((n_c,)), dma, dma((n_c,)), dma((n_c,)),
            dma((n_c, n_z - 1)), dma((n_c, n_z - 1)),
        ] + [dma((n_t,))] * 8,
        compiler_params=pltpu.CompilerParams(
            collective_id=1, has_side_effects=True, vmem_limit_bytes=44 * 2**20
        ),
    )(
        contexts.reshape(n_z, 2, rows, top * slice_ctx),
        att_routes.T,
        att_scores.T,
        att_out_w.reshape(experts * slice_ctx, width),
        resid,
        norm_gain.reshape(1, width),
        router_w.T,
        mlp_routes.T,
        split_rule.T,
        placement,
        cap_blocks,
    )
    hidden = activate(gathered[:, None], w_gate_up)
    n_d = 4
    wide = width // n_d
    group = n_t * cap
    return pl.pallas_call(
        functools.partial(back_kernel, n_e, n_t, n_d, cap),
        out_shape=(jax.ShapeDtypeStruct((rows, width), bf16),) * 2,
        in_specs=[vmem, anywhere] + [vmem] * 4,
        out_specs=(vmem, vmem),
        scratch_shapes=[
            pltpu.VMEM((n_d, unit, wide), bf16),
            pltpu.VMEM((n_d, 2, group, wide), bf16),
            pltpu.VMEM((n_d, 2, group, wide), bf16),
            pltpu.VMEM((n_d, group, wide), bf16),
            pltpu.VMEM((n_d, group, wide), bf16),
            pltpu.VMEM((n_d, 2, group, wide), f32),
            pltpu.VMEM((n_d, n_t, cap, wide), bf16),
            pltpu.VMEM((n_d, n_t, cap, wide), bf16),
            pltpu.VMEM((rows, width), f32),
            dma((n_d,)), dma((n_d,)), dma((n_d,)), dma((n_d,)), dma((n_d,)),
            dma((n_d, n_t - 1)), dma((n_d, n_t - 1)),
        ],
        compiler_params=pltpu.CompilerParams(
            collective_id=2, has_side_effects=True, vmem_limit_bytes=44 * 2**20
        ),
    )(
        hidden.reshape(n_e // 2, 2, group, unit),
        w_down.reshape(unit, width),
        stream,
        gate,
        take,
        final_gain.reshape(1, width),
    )


def choose(*args):
    n_t, n_e = lax.axis_size("tensor"), lax.axis_size("expert")
    resid, placement = args[0], args[9]
    replicas, rows = placement.shape[0], resid.shape[0]
    cap = MAXB * max(1, resid.shape[0] * args[2].shape[1] // (2 * replicas))
    if n_e == 4 and n_t % 2 == 0 and n_t <= 8 and replicas == n_t and cap % 16 == 0 and rows % 64 == 0:
        return fused_device(*args)
    return per_device(*args)


def solution(mesh):
    return jax.shard_map(
        choose,
        mesh=mesh,
        in_specs=(
            P(("expert", "tensor"), None),
            P("expert", "tensor"),
            P("expert", None),
            P("expert", None),
            P(None, "tensor", None),
            P(),
            P(),
            P(("expert", "tensor"), None),
            P(("expert", "tensor"), None),
            P(),
            P(),
            P("tensor", None, None, "expert"),
            P("tensor", "expert", None),
            P(),
        ),
        out_specs=(P(("expert", "tensor"), None), P(("expert", "tensor"), None)),
        check_vma=False,
    )
```

```python
import functools

import jax
import jax.numpy as jnp
from jax import lax
from jax.experimental import pallas as pl
from jax.experimental.pallas import tpu as pltpu
from jax.sharding import PartitionSpec as P

MESH = pl.DeviceIdType.MESH

MAXB = 2


norm_eps = 1e-06


def rms_norm(values, gain):
    scale = lax.rsqrt(jnp.mean(values * values, axis=-1, keepdims=True) + norm_eps)
    return values * scale * gain.astype(values.dtype)


def pair_gates(scores):
    first = jax.nn.silu(scores[:, 0:1] * 0.0) * 0.0 + jax.nn.sigmoid(
        scores[:, 0:1] - scores[:, 1:2]
    )
    first = first[:, 0]
    return jnp.stack([first, 1.0 - first], axis=1)


def activate(shard_piece, w_gate_up):
    both = jnp.einsum(
        "tsecd,sdgf->tsecgf", shard_piece, w_gate_up, preferred_element_type=jnp.float32
    )
    hidden = (jax.nn.silu(both[:, :, :, :, 0, :]) * both[:, :, :, :, 1, :]).astype(jnp.bfloat16)
    hidden = jnp.transpose(hidden, (0, 2, 3, 1, 4))
    return hidden.reshape(
        hidden.shape[0] * hidden.shape[1] * hidden.shape[2], hidden.shape[3], hidden.shape[4]
    )


def per_device(
    resid,
    contexts,
    att_routes,
    att_scores,
    att_out_w,
    norm_gain,
    router_w,
    mlp_routes,
    split_rule,
    placement,
    cap_blocks,
    w_gate_up,
    w_down,
    final_gain,
):
    n_tensor = lax.axis_size("tensor")
    row_count = resid.shape[0]
    model_width = resid.shape[1]
    group_rows = contexts.shape[0]
    att_experts = att_out_w.shape[0]
    slice_ctx = att_out_w.shape[1]
    top_count = att_routes.shape[1]
    gate_att = pair_gates(att_scores)
    chosen = (
        att_routes[:, :, None] == jnp.arange(att_experts, dtype=jnp.int32)[None, None, :]
    ).astype(jnp.float32)
    weighted = chosen * gate_att[:, :, None]
    context_part = contexts.reshape(group_rows, slice_ctx, top_count).astype(jnp.float32)
    mixed = (
        jnp.einsum("tke,tck->tec", weighted, context_part)
        .astype(jnp.bfloat16)
        .reshape(group_rows, att_experts * slice_ctx)
    )
    weight_flat = att_out_w.reshape(att_experts * slice_ctx, model_width)
    row_block = mixed
    attention = lax.psum_scatter(
        jnp.dot(row_block, weight_flat, preferred_element_type=jnp.float32).astype(jnp.bfloat16),
        "tensor",
        scatter_dimension=0,
        tiled=True,
    ).astype(jnp.float32)
    stream = (resid.astype(jnp.float32) + attention).astype(jnp.bfloat16)
    normed = rms_norm(stream.astype(jnp.float32), norm_gain).astype(jnp.bfloat16)
    logits = jnp.dot(normed, router_w, preferred_element_type=jnp.float32)
    gate_mlp = pair_gates(jnp.take_along_axis(logits, mlp_routes, axis=1))
    replicas = placement.shape[0]
    slots = w_gate_up.shape[0]
    expert_total = router_w.shape[1]
    block_rows = max(1, row_count * top_count // (2 * replicas))
    capacity_rows = MAXB * block_rows
    slot_ids = jnp.arange(replicas, dtype=jnp.int32)
    expert_ids = jnp.arange(expert_total, dtype=jnp.int32)
    copies = jnp.sum((placement[None, :] == expert_ids[:, None]).astype(jnp.int32), axis=1)
    earlier = jnp.sum(
        (
            (placement[None, :] == placement[:, None]) & (slot_ids[None, :] < slot_ids[:, None])
        ).astype(jnp.int32),
        axis=1,
    )
    route_onehot = (mlp_routes[:, :, None] == expert_ids[None, None, :]).astype(jnp.int32)
    route_copies = jnp.sum(route_onehot * copies[None, None, :], axis=2)
    replica_rank = jnp.remainder(split_rule, route_copies)
    match = (
        (placement[None, None, :] == mlp_routes[:, :, None])
        & (earlier[None, None, :] == replica_rank[:, :, None])
    ).astype(jnp.int32)
    replica_slot = jnp.sum(match * slot_ids[None, None, :], axis=2)
    capacity = jnp.sum(match * cap_blocks[None, None, :], axis=2) * block_rows
    flat_match = match.reshape(row_count * top_count, replicas)
    before = jnp.cumsum(flat_match, axis=0) - flat_match
    arrival = jnp.sum(before * flat_match, axis=1).reshape(row_count, top_count)
    is_kept = arrival < capacity
    holder = replica_slot // slots
    within = replica_slot % slots
    position = within * (n_tensor * capacity_rows) + holder * capacity_rows + arrival
    position = jnp.where(is_kept, position, -1)
    buffer_rows = slots * n_tensor * capacity_rows
    placer = jnp.sum(
        (jnp.arange(buffer_rows, dtype=jnp.int32)[:, None, None] == position[None, :, :]).astype(
            jnp.bfloat16
        ),
        axis=2,
    )
    send_rows = jnp.dot(placer, normed, preferred_element_type=jnp.float32).astype(jnp.bfloat16)
    send_rows = send_rows.reshape(slots, n_tensor, capacity_rows, model_width)
    landed = lax.all_to_all(send_rows, "tensor", split_axis=1, concat_axis=1, tiled=True)
    arrived = lax.all_gather(landed[None], "expert", axis=0, tiled=True)
    hidden = activate(arrived, w_gate_up)
    row_block = hidden
    summed = lax.psum_scatter(
        jnp.einsum("bsf,sfd->bsd", row_block, w_down, preferred_element_type=jnp.float32).astype(
            jnp.bfloat16
        ),
        "expert",
        scatter_dimension=0,
        tiled=True,
    )
    results = summed.reshape(n_tensor, capacity_rows, slots, model_width)
    returned = lax.all_to_all(results, "tensor", split_axis=0, concat_axis=0, tiled=True)
    flat_back = returned.reshape(n_tensor * capacity_rows * slots, model_width)
    back_index = jnp.where(is_kept, holder * (capacity_rows * slots) + arrival * slots + within, 0)
    fetched = (
        jnp.take(flat_back, back_index.reshape(-1), axis=0)
        .reshape(row_count, top_count, model_width)
        .astype(jnp.float32)
    )
    factors = gate_mlp * is_kept.astype(jnp.float32)
    expert_mix = fetched[:, 0, :] * factors[:, 0:1] + fetched[:, 1, :] * factors[:, 1:2]
    after = stream.astype(jnp.float32) + expert_mix
    return (after.astype(jnp.bfloat16), rms_norm(after, final_gain).astype(jnp.bfloat16))


def greet(n_e, n_t):
    e, t = lax.axis_index("expert"), lax.axis_index("tensor")
    barrier = pltpu.get_barrier_semaphore()
    for d in range(1, n_t):
        pl.semaphore_signal(
            barrier, inc=1, device_id=(e, lax.rem(t + d, n_t)), device_id_type=MESH
        )
    for d in range(1, n_e):
        pl.semaphore_signal(
            barrier, inc=1, device_id=(lax.rem(e + d, n_e), t), device_id_type=MESH
        )
    return barrier, n_t + n_e - 2


def send(src, dst, send_sem, recv_sem, device):
    return pltpu.make_async_remote_copy(
        src_ref=src,
        dst_ref=dst,
        send_sem=send_sem,
        recv_sem=recv_sem,
        device_id=device,
        device_id_type=MESH,
    )


def column(row):
    n = row.shape[1]
    i = lax.broadcasted_iota(jnp.int32, (n, n), 0)
    j = lax.broadcasted_iota(jnp.int32, (n, n), 1)
    return jnp.sum(jnp.where(i == j, row, 0.0), axis=1, keepdims=True)


def assign(routes, splits, place_ref, blocks_ref, block_rows, cap):
    replicas = place_ref.shape[0]
    place = [place_ref[r] for r in range(replicas)]
    limit = [(blocks_ref[r] * block_rows).astype(jnp.float32) for r in range(replicas)]
    earlier = [
        sum(((place[q] == place[r]).astype(jnp.int32) for q in range(r)), jnp.int32(0)).astype(
            jnp.float32
        )
        for r in range(replicas)
    ]
    place = [p.astype(jnp.float32) for p in place]
    rows = routes[0].shape[0]
    lane = lax.broadcasted_iota(jnp.int32, (rows, replicas), 1)
    matches, slots, limits = [], [], []
    for route, split in zip(routes, splits):
        held_by = [(route == p).astype(jnp.float32) for p in place]
        copies = sum(held_by)
        rank = split - copies * jnp.floor((split + 0.5) / copies)
        hits = [h * (rank == q).astype(jnp.float32) for h, q in zip(held_by, earlier)]
        match = jnp.zeros((rows, replicas), jnp.float32)
        for r, hit in enumerate(hits):
            match += jnp.where(lane == r, hit, 0.0)
        matches.append(match)
        slots.append(sum(hit * float(r) for r, hit in enumerate(hits)))
        limits.append(sum(hit * m for hit, m in zip(hits, limit)))
    i = lax.broadcasted_iota(jnp.int32, (rows, rows), 0)
    j = lax.broadcasted_iota(jnp.int32, (rows, rows), 1)
    lower = (j < i).astype(jnp.float32)
    before = jnp.dot(lower, matches[0] + matches[1], preferred_element_type=jnp.float32)
    befores = (before, before + matches[0])
    spot = lax.broadcasted_iota(jnp.int32, (rows, replicas * cap), 1).astype(jnp.float32)
    taken = []
    for k in range(2):
        arrival = jnp.sum(befores[k] * matches[k], axis=1, keepdims=True)
        position = jnp.where(arrival < limits[k], slots[k] * cap + arrival, -1.0)
        taken.append((spot == position).astype(jnp.float32))
    return taken


def front_kernel(
    n_e, n_t, n_c, cap,
    ctx_hbm, routes_hbm, scores_hbm, w_hbm, resid_hbm, gain_hbm, router_hbm,
    chosen_hbm, split_hbm, place_hbm, blocks_hbm,
    rows_hbm, stream_ref, gate_ref, take_ref,
    ctx_ref, routes_ref, scores_ref, resid_ref, gain_ref, router_ref,
    chosen_ref, split_ref, place_ref, blocks_ref, in_sem,
    w, mixed, q_send, q_recv, s_send, s_recv, own, d_send, held,
    w_sem, out_sem, qs, qr, ss, sr, ds, dr, xs, xr, cs, cr, fs, fr,
):
    e, t = lax.axis_index("expert"), lax.axis_index("tensor")
    n_z = n_t // 2
    z, y = t // 2, lax.rem(t, 2)
    other = t + 1 - 2 * y
    cross, sibling = lax.rem(e + 2, 4), e + 1 - 2 * lax.rem(e, 2)
    rows = resid_ref.shape[0]
    cols = w.shape[2]
    slice_ctx = ctx_ref.shape[3] // 2
    experts = w.shape[1] // slice_ctx

    def w_copy(c):
        return pltpu.make_async_copy(
            w_hbm.at[:, pl.ds(c * cols, cols)], w.at[c], w_sem.at[c]
        )

    loads = [
        pltpu.make_async_copy(far, near, in_sem.at[i])
        for i, (far, near) in enumerate(
            (
                (ctx_hbm, ctx_ref),
                (routes_hbm, routes_ref),
                (scores_hbm, scores_ref),
                (resid_hbm, resid_ref),
                (gain_hbm, gain_ref),
                (router_hbm, router_ref),
                (chosen_hbm, chosen_ref),
                (split_hbm, split_ref),
                (place_hbm, place_ref),
                (blocks_hbm, blocks_ref),
            )
        )
    ]
    for load in loads:
        load.start()
    for c in range(n_c):
        w_copy(c).start()
    barrier, guests = greet(n_e, n_t)
    for load in loads:
        load.wait()

    j = lax.broadcasted_iota(jnp.int32, (2 * slice_ctx, slice_ctx), 0)
    f = lax.broadcasted_iota(jnp.int32, (2 * slice_ctx, slice_ctx), 1)
    even = (j == 2 * f).astype(jnp.float32).astype(jnp.bfloat16)
    odd = (j == 2 * f + 1).astype(jnp.float32).astype(jnp.bfloat16)

    def mix_block(zz, carry):
        ctx = ctx_ref[zz].reshape(2 * rows, 2 * slice_ctx)
        first = jnp.dot(ctx, even, preferred_element_type=jnp.float32)
        second = jnp.dot(ctx, odd, preferred_element_type=jnp.float32)
        at = pl.ds(pl.multiple_of(zz * 2 * rows, 2 * rows), 2 * rows)
        scores = scores_ref[:, at]
        routes = routes_ref[:, at].astype(jnp.float32)
        g0 = column(jax.nn.sigmoid(scores[0:1] - scores[1:2]))
        r0, r1 = column(routes[0:1]), column(routes[1:2])
        first = first * g0
        second = second * (1.0 - g0)
        for x in range(experts):
            value = jnp.where(r0 == x, first, 0.0) + jnp.where(r1 == x, second, 0.0)
            mixed[zz, :, :, x * slice_ctx : (x + 1) * slice_ctx] = value.astype(
                jnp.bfloat16
            ).reshape(2, rows, slice_ctx)
        return carry

    lax.fori_loop(0, n_z, mix_block, 0)
    pl.semaphore_wait(barrier, guests)

    def q_copy(c):
        return send(q_send.at[c], q_recv.at[c], qs.at[c], qr.at[c], (e, other))

    def s_copy(c, d):
        to = lax.rem(z + d, n_z) * 2 + y
        return send(s_send.at[c, d - 1], s_recv.at[c, d - 1], ss.at[c, d - 1], sr.at[c, d - 1], (e, to))

    def pair_step(c, carry):
        w_copy(c).wait()
        block = mixed[:, 1 - y].reshape(n_z * rows, w.shape[1])
        part = jnp.dot(block, w[c], preferred_element_type=jnp.float32)
        q_send[c] = part.astype(jnp.bfloat16).reshape(n_z, rows, cols)
        q_copy(c).start()
        return carry

    lax.fori_loop(0, n_c, pair_step, 0)

    routes = [column(chosen_ref[k : k + 1].astype(jnp.float32)) for k in range(2)]
    splits = [column(split_ref[k : k + 1].astype(jnp.float32)) for k in range(2)]
    taken = assign(routes, splits, place_ref, blocks_ref, cap // MAXB, cap)
    for k in range(2):
        take_ref[k] = taken[k].astype(jnp.bfloat16)

    def own_step(c, carry):
        block = mixed[:, y].reshape(n_z * rows, w.shape[1])
        own[c] = jnp.dot(block, w[c], preferred_element_type=jnp.float32).reshape(n_z, rows, cols)
        q_copy(c).wait_recv()
        for d in range(1, n_z):
            to = lax.rem(z + d, n_z)
            s_send[c, d - 1] = (own[c, to] + q_recv[c, to].astype(jnp.float32)).astype(jnp.bfloat16)
            s_copy(c, d).start()
        return carry

    lax.fori_loop(0, n_c, own_step, 0)

    square = jnp.zeros((rows, 1), jnp.float32)
    for c in range(n_c):
        total = own[c, z] + q_recv[c, z].astype(jnp.float32)
        for d in range(1, n_z):
            s_copy(c, d).wait_recv()
            total += s_recv[c, d - 1].astype(jnp.float32)
        at = slice(c * cols, (c + 1) * cols)
        piece = (resid_ref[:, at].astype(jnp.float32) + total).astype(jnp.bfloat16)
        stream_ref[:, at] = piece
        wide = piece.astype(jnp.float32)
        square += jnp.sum(wide * wide, axis=1, keepdims=True)
    width = resid_ref.shape[1]
    scale = lax.rsqrt(square / width + norm_eps)
    normed = (
        stream_ref[...].astype(jnp.float32) * scale * gain_ref[...].astype(jnp.float32)
    ).astype(jnp.bfloat16)
    picked = lax.dot_general(
        (taken[0] + taken[1]).astype(jnp.bfloat16),
        normed,
        (((0,), (0,)), ((), ())),
        preferred_element_type=jnp.float32,
    )
    d_send[...] = picked.astype(jnp.bfloat16).reshape(n_t, cap, width)

    def d_copy(d):
        to = lax.rem(t + d, n_t)
        return send(d_send.at[to], held.at[e, t], ds.at[d], dr.at[d], (e, to))

    for d in range(1, n_t):
        d_copy(d).start()
    held[e, t] = d_send[t]

    def x_copy(d):
        src = held.at[e, lax.rem(t + n_t - d, n_t)]
        return send(src, src, xs.at[d], xr.at[d], (cross, t))

    def c_copy(d):
        src = held.at[e, lax.rem(t + n_t - d, n_t)]
        return send(src, src, cs.at[d], cr.at[d], (sibling, t))

    def f_copy(d):
        src = held.at[cross, lax.rem(t + n_t - d, n_t)]
        return send(src, src, fs.at[d], fr.at[d], (sibling, t))

    for d in range(n_t):
        if d:
            d_copy(d).wait_recv()
        x_copy(d).start()
        c_copy(d).start()

    logits = lax.dot_general(
        normed, router_ref[...], (((1,), (1,)), ((), ())), preferred_element_type=jnp.float32
    )
    expert = lax.broadcasted_iota(jnp.int32, logits.shape, 1).astype(jnp.float32)
    pick = (expert == routes[0]).astype(jnp.float32) - (expert == routes[1]).astype(jnp.float32)
    gap = jnp.sum(logits * pick, axis=1, keepdims=True)
    gate_ref[...] = jnp.broadcast_to(jax.nn.sigmoid(gap), gate_ref.shape)

    for d in range(n_t):
        x_copy(d).wait_recv()
        f_copy(d).start()
    for d in range(n_t):
        c_copy(d).wait_recv()
        f_copy(d).wait_recv()
    out = pltpu.make_async_copy(held, rows_hbm, out_sem)
    out.start()

    def q_end(c, carry):
        q_copy(c).wait_send()
        for d in range(1, n_z):
            s_copy(c, d).wait_send()
        return carry

    lax.fori_loop(0, n_c, q_end, 0)
    for d in range(n_t):
        if d:
            d_copy(d).wait_send()
        x_copy(d).wait_send()
        c_copy(d).wait_send()
        f_copy(d).wait_send()
    out.wait()


def back_kernel(
    n_e, n_t, n_c, cap,
    hidden_ref, w_hbm, stream_ref, gate_ref, take_ref, gain_ref,
    out_ref, normal_ref,
    w, a_send, a_recv, x_send, x_recv, own, r_send, back, after,
    w_sem, as_, ar, xs, xr, rs, rr,
):
    e, t = lax.axis_index("expert"), lax.axis_index("tensor")
    chip, core = e // 2, lax.rem(e, 2)
    cross, sibling = lax.rem(e + 2, 4), e + 1 - 2 * core
    rows = stream_ref.shape[0]
    cols = w.shape[2]
    group = n_t * cap

    def w_copy(c):
        return pltpu.make_async_copy(
            w_hbm.at[:, pl.ds(c * cols, cols)], w.at[c], w_sem.at[c]
        )

    for c in range(n_c):
        w_copy(c).start()
    pl.semaphore_wait(*greet(n_e, n_t))

    def a_copy(c):
        return send(a_send.at[c], a_recv.at[c], as_.at[c], ar.at[c], (sibling, t))

    def x_copy(c):
        return send(x_send.at[c], x_recv.at[c], xs.at[c], xr.at[c], (cross, t))

    def r_copy(c, d):
        to = lax.rem(t + d, n_t)
        return send(r_send.at[c, to], back.at[c, t], rs.at[c, d - 1], rr.at[c, d - 1], (e, to))

    def sibling_step(c, carry):
        w_copy(c).wait()
        block = hidden_ref[:, 1 - core].reshape(2 * group, w.shape[1])
        part = jnp.dot(block, w[c], preferred_element_type=jnp.float32)
        a_send[c] = part.astype(jnp.bfloat16).reshape(2, group, cols)
        a_copy(c).start()
        return carry

    lax.fori_loop(0, n_c, sibling_step, 0)

    def own_step(c, carry):
        block = hidden_ref[:, core].reshape(2 * group, w.shape[1])
        own[c] = jnp.dot(block, w[c], preferred_element_type=jnp.float32).reshape(2, group, cols)
        a_copy(c).wait_recv()
        x_send[c] = (own[c, 1 - chip] + a_recv[c, 1 - chip].astype(jnp.float32)).astype(jnp.bfloat16)
        x_copy(c).start()
        return carry

    lax.fori_loop(0, n_c, own_step, 0)

    def return_step(c, carry):
        x_copy(c).wait_recv()
        total = own[c, chip] + a_recv[c, chip].astype(jnp.float32) + x_recv[c].astype(jnp.float32)
        r_send[c] = total.astype(jnp.bfloat16).reshape(n_t, cap, cols)
        for d in range(1, n_t):
            r_copy(c, d).start()
        back[c, t] = r_send[c, t]
        return carry

    lax.fori_loop(0, n_c, return_step, 0)

    first = gate_ref[:, 0:1]
    square = jnp.zeros((rows, 1), jnp.float32)
    for c in range(n_c):
        for d in range(1, n_t):
            r_copy(c, d).wait_recv()
        came = back[c].reshape(group, cols)
        one = jnp.dot(take_ref[0], came, preferred_element_type=jnp.float32)
        two = jnp.dot(take_ref[1], came, preferred_element_type=jnp.float32)
        at = slice(c * cols, (c + 1) * cols)
        value = stream_ref[:, at].astype(jnp.float32) + (one * first + two * (1.0 - first))
        after[:, at] = value
        out_ref[:, at] = value.astype(jnp.bfloat16)
        square += jnp.sum(value * value, axis=1, keepdims=True)
    scale = lax.rsqrt(square / stream_ref.shape[1] + norm_eps)
    normal_ref[...] = (after[...] * scale * gain_ref[...].astype(jnp.float32)).astype(jnp.bfloat16)

    def end(c, carry):
        a_copy(c).wait_send()
        x_copy(c).wait_send()
        for d in range(1, n_t):
            r_copy(c, d).wait_send()
        return carry

    lax.fori_loop(0, n_c, end, 0)


def fused_device(
    resid, contexts, att_routes, att_scores, att_out_w, norm_gain, router_w, mlp_routes, split_rule,
    placement, cap_blocks, w_gate_up, w_down, final_gain,
):
    n_t, n_e = lax.axis_size("tensor"), lax.axis_size("expert")
    rows, width = resid.shape
    n_z = n_t // 2
    experts, slice_ctx = att_out_w.shape[0], att_out_w.shape[1]
    top = att_routes.shape[1]
    expert_total = router_w.shape[1]
    cap = MAXB * max(1, rows * top // (2 * placement.shape[0]))
    unit = w_down.shape[1]
    bf16, f32, dma = jnp.bfloat16, jnp.float32, pltpu.SemaphoreType.DMA
    vmem, anywhere = pl.BlockSpec(memory_space=pltpu.VMEM), pl.BlockSpec(memory_space=pl.ANY)

    n_c = 8
    cols = width // n_c
    gathered, stream, gate, take = pl.pallas_call(
        functools.partial(front_kernel, n_e, n_t, n_c, cap),
        out_shape=(
            jax.ShapeDtypeStruct((n_e, n_t, cap, width), bf16),
            jax.ShapeDtypeStruct((rows, width), bf16),
            jax.ShapeDtypeStruct((rows, 128), f32),
            jax.ShapeDtypeStruct((top, rows, n_t * cap), bf16),
        ),
        in_specs=[anywhere] * 11,
        out_specs=(anywhere, vmem, vmem, vmem),
        scratch_shapes=[
            pltpu.VMEM((n_z, 2, rows, top * slice_ctx), bf16),
            pltpu.VMEM((top, n_t * rows), jnp.int32),
            pltpu.VMEM((top, n_t * rows), f32),
            pltpu.VMEM((rows, width), bf16),
            pltpu.VMEM((1, width), bf16),
            pltpu.VMEM((expert_total, width), bf16),
            pltpu.VMEM((top, rows), jnp.int32),
            pltpu.VMEM((top, rows), jnp.int32),
            pltpu.SMEM(placement.shape, jnp.int32),
            pltpu.SMEM(cap_blocks.shape, jnp.int32),
            dma((10,)),
            pltpu.VMEM((n_c, experts * slice_ctx, cols), bf16),
            pltpu.VMEM((n_z, 2, rows, experts * slice_ctx), bf16),
            pltpu.VMEM((n_c, n_z, rows, cols), bf16),
            pltpu.VMEM((n_c, n_z, rows, cols), bf16),
            pltpu.VMEM((n_c, n_z - 1, rows, cols), bf16),
            pltpu.VMEM((n_c, n_z - 1, rows, cols), bf16),
            pltpu.VMEM((n_c, n_z, rows, cols), f32),
            pltpu.VMEM((n_t, cap, width), bf16),
            pltpu.VMEM((n_e, n_t, cap, width), bf16),
            dma((n_c,)), dma, dma((n_c,)), dma((n_c,)),
            dma((n_c, n_z - 1)), dma((n_c, n_z - 1)),
        ] + [dma((n_t,))] * 8,
        compiler_params=pltpu.CompilerParams(
            collective_id=1, has_side_effects=True, vmem_limit_bytes=60 * 2**20
        ),
    )(
        contexts.reshape(n_z, 2, rows, top * slice_ctx),
        att_routes.T,
        att_scores.T,
        att_out_w.reshape(experts * slice_ctx, width),
        resid,
        norm_gain.reshape(1, width),
        router_w.T,
        mlp_routes.T,
        split_rule.T,
        placement,
        cap_blocks,
    )
    hidden = activate(gathered[:, None], w_gate_up)
    n_d = 4
    wide = width // n_d
    group = n_t * cap
    return pl.pallas_call(
        functools.partial(back_kernel, n_e, n_t, n_d, cap),
        out_shape=(jax.ShapeDtypeStruct((rows, width), bf16),) * 2,
        in_specs=[vmem, anywhere] + [vmem] * 4,
        out_specs=(vmem, vmem),
        scratch_shapes=[
            pltpu.VMEM((n_d, unit, wide), bf16),
            pltpu.VMEM((n_d, 2, group, wide), bf16),
            pltpu.VMEM((n_d, 2, group, wide), bf16),
            pltpu.VMEM((n_d, group, wide), bf16),
            pltpu.VMEM((n_d, group, wide), bf16),
            pltpu.VMEM((n_d, 2, group, wide), f32),
            pltpu.VMEM((n_d, n_t, cap, wide), bf16),
            pltpu.VMEM((n_d, n_t, cap, wide), bf16),
            pltpu.VMEM((rows, width), f32),
            dma((n_d,)), dma((n_d,)), dma((n_d,)), dma((n_d,)), dma((n_d,)),
            dma((n_d, n_t - 1)), dma((n_d, n_t - 1)),
        ],
        compiler_params=pltpu.CompilerParams(
            collective_id=2, has_side_effects=True, vmem_limit_bytes=44 * 2**20
        ),
    )(
        hidden.reshape(n_e // 2, 2, group, unit),
        w_down.reshape(unit, width),
        stream,
        gate,
        take,
        final_gain.reshape(1, width),
    )


def choose(*args):
    n_t, n_e = lax.axis_size("tensor"), lax.axis_size("expert")
    resid, placement = args[0], args[9]
    replicas, rows = placement.shape[0], resid.shape[0]
    cap = MAXB * max(1, resid.shape[0] * args[2].shape[1] // (2 * replicas))
    if n_e == 4 and n_t % 2 == 0 and n_t <= 8 and replicas == n_t and cap % 16 == 0 and rows % 64 == 0:
        return fused_device(*args)
    return per_device(*args)


def solution(mesh):
    return jax.shard_map(
        choose,
        mesh=mesh,
        in_specs=(
            P(("expert", "tensor"), None),
            P("expert", "tensor"),
            P("expert", None),
            P("expert", None),
            P(None, "tensor", None),
            P(),
            P(),
            P(("expert", "tensor"), None),
            P(("expert", "tensor"), None),
            P(),
            P(),
            P("tensor", None, None, "expert"),
            P("tensor", "expert", None),
            P(),
        ),
        out_specs=(P(("expert", "tensor"), None), P(("expert", "tensor"), None)),
        check_vma=False,
    )
```
